256 devices in a mesh: dp: 8 (over y, z_lo), tensor: 32 (over z_hi, x, core).
Axes of the slice: x: 4, y: 4, z: 8 (z_hi: 4, z_lo: 2; z = z_hi * 2 + z_lo), core: 2. Of those that a mesh axis runs over, the one named last changes fastest.
Arguments:
- query_latent: bfloat16 [2, 512, 1536], P(None, ('dp', 'tensor')), may hold values from -6 to 6
- fresh_latent: bfloat16 [2, 512, 576], P(None, ('dp', 'tensor')), may hold values from -4 to 4
- stream: bfloat16 [2, 512, 7168], P(None, ('dp', 'tensor')), may hold values from -4 to 4
- lengths: int32 [512], P(('dp', 'tensor')), may hold values from 128 to 512, as said below
- latent_cache: bfloat16 [512, 512, 576], P(('dp', 'tensor')), may hold values from -300 to 300
- w_qb: bfloat16 [1536, 24576], P('dp', 'tensor'), may hold values from -0.15625 to 0.15625
- w_uk: bfloat16 [128, 128, 512], P('tensor'), may hold values from -0.5 to 0.5
- w_uv: bfloat16 [128, 512, 128], P('tensor'), may hold values from -0.25 to 0.25
- w_o: bfloat16 [16384, 7168], P('tensor'), may hold values from -0.1875 to 0.1875
- norm_gain: bfloat16 [7168], replicated, may hold values from 0.25 to 1.75
- w_gate: bfloat16 [7168, 9216], P('dp', 'tensor'), may hold values from -0.0625 to 0.0625
- w_up: bfloat16 [7168, 9216], P('dp', 'tensor'), may hold values from -0.0625 to 0.0625
- w_down: bfloat16 [9216, 7168], P('tensor', 'dp'), may hold values from -0.0625 to 0.0625
Outputs:
- layer_out: bfloat16 [2, 512, 7168], P(None, ('dp', 'tensor'))
The draws below stay inside these ranges and needn't reach their ends.
Inputs may be any that keep to these rules, and one draw needn't show every extreme that they name: Row n attends to its first lengths[n] cache slots; some row fills all 512 slots and some row exactly 128.
All inputs are finite; a program needn't handle non-finite values.
Results may differ from the reference program's by a relative error of at most 0.035.
Values may be sent and summed in bfloat16 or wider, within the bound.
No kernel may reach another device: no remote copies, remote signals or barrier semaphores. Data moves between devices by JAX's collectives and lax.ppermute only.
A program may use at most 128 MiB of HBM per device.

```python
import math
import jax
import jax.numpy as jnp
from jax import lax

D = 7168
HEADS = 128
NOPE = 128
ROPE = 64
LATENT = 512
VHEAD = 128
QLAT = 1536
FF = 9216
STEPS = 2
ROWS_DEV = 2
CACHE = 512
ROWS = 512
N_TENSOR = 32


def draw_lengths(key, part):
    key = jax.random.fold_in(key, 11)
    first_key, second_key = jax.random.split(key)
    drawn = jax.random.randint(first_key, (ROWS,), CACHE // 4, CACHE + 1)
    order = jax.random.permutation(second_key, ROWS)
    drawn = drawn.at[order[0]].set(CACHE)
    drawn = drawn.at[order[1]].set(CACHE // 4)
    return drawn.astype(jnp.int32)


def draw_latent_cache(key, part):
    key = jax.random.fold_in(key, 23)
    shape = (ROWS, CACHE, LATENT + ROPE)
    values = jnp.clip(jax.random.normal(key, shape, jnp.float32), -4.0, 4.0)
    return values.astype(jnp.bfloat16)


def block_scale(rng, extent, pieces, least, high):
    def one(axis_at, blocks):
        heights = jax.random.uniform(jax.random.fold_in(jax.random.fold_in(rng, 6), axis_at), (blocks,), jnp.float32, least / len(pieces), high / len(pieces))
        return jnp.repeat(jnp.exp(heights), extent[axis_at] // blocks).reshape((-1,) + (1,) * (len(extent) - axis_at - 1))

    level = one(*pieces[0])
    for cut in pieces[1:]:
        level = level * one(*cut)
    return level


def bell_draw(own_key, dims, scale, limit, cuts=(), dtype=jnp.bfloat16):
    result = scale * jax.random.normal(own_key, dims, jnp.float32)
    if cuts:
        result = result * block_scale(own_key, dims, cuts, -0.22, 0.18)
    return jnp.clip(result, -limit, limit).astype(dtype)


def setup_inputs(seed: int = 0) -> dict:
    splits = jax.random.split(jax.random.key(seed), 14)
    return {
        "query_latent": bell_draw(splits[0], (STEPS, ROWS, QLAT), 1.0, 6.0, ((1, 256),)),
        "fresh_latent": bell_draw(splits[1], (STEPS, ROWS, LATENT + ROPE), 1.0, 4.0, ((1, 256),)),
        "stream": bell_draw(splits[2], (STEPS, ROWS, D), 0.5, 4.0, ((1, 256),)),
        "lengths": draw_lengths(jax.random.fold_in(splits[13], 71), 0),
        "latent_cache": draw_latent_cache(jax.random.fold_in(splits[13], 71), 0),
        "w_qb": bell_draw(splits[5], (QLAT, HEADS * (NOPE + ROPE)), QLAT ** -0.5, 0.15625, ((0, 8), (1, 32))),
        "w_uk": bell_draw(splits[6], (HEADS, NOPE, LATENT), NOPE ** -0.5, 0.5, ((0, 32),)),
        "w_uv": bell_draw(splits[7], (HEADS, LATENT, VHEAD), LATENT ** -0.5, 0.25, ((0, 32),)),
        "w_o": bell_draw(splits[8], (HEADS * VHEAD, D), (HEADS * VHEAD // 16) ** -0.5, 0.1875, ((0, 32),)),
        "norm_gain": jnp.clip(1.0 + 0.15 * jax.random.normal(splits[9], (D,), jnp.float32), 0.25, 1.75).astype(jnp.bfloat16),
        "w_gate": bell_draw(splits[10], (D, FF), D ** -0.5, 0.0625, ((0, 8), (1, 32))),
        "w_up": bell_draw(splits[11], (D, FF), D ** -0.5, 0.0625, ((0, 8), (1, 32))),
        "w_down": bell_draw(splits[12], (FF, D), FF ** -0.5, 0.0625, ((0, 32), (1, 8))),
    }


def rotate_pairs(pairs, position):
    half_width = pairs.shape[-1] // 2
    ladder = jnp.arange(half_width).astype(jnp.float32)
    frequency = jnp.exp(ladder * (-2.0 * math.log(10000.0) / pairs.shape[-1]))
    angle = position.astype(jnp.float32)[:, None] * frequency[None, :]
    cosine = jnp.cos(angle)[:, None, :]
    sine_part = jnp.sin(angle)[:, None, :]
    first = pairs[..., :half_width].astype(jnp.float32)
    second = pairs[..., half_width:].astype(jnp.float32)
    return jnp.concatenate([first * cosine - second * sine_part, first * sine_part + second * cosine], axis=-1)

def attend_block(query, row_lengths, cache_rows, newest):
    scale = (NOPE + ROPE) ** (-0.5)
    queries_wide = query.astype(jnp.float32)
    scores = jnp.einsum('rhc,rlc->rhl', queries_wide, cache_rows.astype(jnp.float32)) * scale
    slots = jnp.arange(cache_rows.shape[1])
    scores = jnp.where(slots[None, None, :] < row_lengths[:, None, None], scores, -jnp.inf)
    own_scores = jnp.einsum('rhc,rtc->rht', queries_wide, newest.astype(jnp.float32)) * scale
    joined = jnp.concatenate([scores, own_scores], axis=-1)
    peak = lax.optimization_barrier(jnp.max(joined, axis=-1, keepdims=True))
    weights = jnp.exp(joined - peak)
    probs = (weights / lax.optimization_barrier(jnp.sum(weights, axis=-1, keepdims=True))).astype(jnp.bfloat16)
    values = jnp.concatenate([cache_rows[..., :LATENT], newest[..., :LATENT]], axis=1).astype(jnp.float32)
    return jnp.einsum('rhl,rlc->rhc', probs.astype(jnp.float32), values).astype(jnp.bfloat16)

def rms_scale(mixed, norm_gain):
    wide = mixed.astype(jnp.float32)
    factor = lax.rsqrt(lax.optimization_barrier(jnp.mean(wide * wide, axis=-1, keepdims=True)) + 1e-06)
    return (wide * factor * norm_gain.astype(jnp.float32)).astype(jnp.bfloat16)

def reference(query_latent, fresh_latent, stream, lengths, latent_cache, w_qb, w_uk, w_uv, w_o, norm_gain, w_gate, w_up, w_down):
    heads_group = HEADS // N_TENSOR
    blocks = ROWS // ROWS_DEV
    outputs = []
    for step_index in range(STEPS):
        projected = jnp.dot(query_latent[step_index], w_qb, preferred_element_type=jnp.float32).astype(jnp.bfloat16)
        projected = projected.reshape(ROWS, HEADS, NOPE + ROPE)
        absorbed = jnp.einsum('nhd,hdc->nhc', projected[..., :NOPE].astype(jnp.float32), w_uk.astype(jnp.float32)).astype(jnp.bfloat16)
        rotated = rotate_pairs(projected[..., NOPE:], lengths + step_index).astype(jnp.bfloat16)
        query = jnp.concatenate([absorbed, rotated], axis=-1)
        newest = jnp.swapaxes(fresh_latent[:step_index + 1], 0, 1)

        def run_block(parts):
            return attend_block(parts[0], parts[1], parts[2], parts[3])
        attended = lax.map(run_block, (query.reshape(blocks, ROWS_DEV, HEADS, LATENT + ROPE), lengths.reshape(blocks, ROWS_DEV), latent_cache.reshape(blocks, ROWS_DEV, CACHE, LATENT + ROPE), newest.reshape(blocks, ROWS_DEV, step_index + 1, LATENT + ROPE)))
        attended = attended.reshape(ROWS, HEADS, LATENT)
        head_values = jnp.einsum('nhc,hcv->nhv', attended.astype(jnp.float32), w_uv.astype(jnp.float32)).astype(jnp.bfloat16)
        grouped = jnp.swapaxes(head_values.reshape(ROWS, N_TENSOR, heads_group * VHEAD), 0, 1)
        weight_groups = w_o.reshape(N_TENSOR, heads_group * VHEAD, D)

        def add_group(carry, pair):
            part = jnp.dot(pair[0], pair[1], preferred_element_type=jnp.float32).astype(jnp.bfloat16)
            part = lax.optimization_barrier(part)
            return (carry + part.astype(jnp.float32), None)
        attention_out, _ = lax.scan(add_group, jnp.zeros((ROWS, D), jnp.float32), (grouped, weight_groups))
        mixed = (stream[step_index].astype(jnp.float32) + attention_out).astype(jnp.bfloat16)
        normed = rms_scale(mixed, norm_gain)
        gate_value = jnp.dot(normed, w_gate, preferred_element_type=jnp.float32)
        up_value = jnp.dot(normed, w_up, preferred_element_type=jnp.float32)
        hidden = (jax.nn.silu(gate_value) * up_value).astype(jnp.bfloat16)
        ffn_value = jnp.dot(hidden, w_down, preferred_element_type=jnp.float32)
        outputs.append((mixed.astype(jnp.float32) + ffn_value).astype(jnp.bfloat16))
    return jnp.stack(outputs, axis=0)
```

```python
import math

import jax
import jax.numpy as jnp
from jax import lax
from jax.sharding import PartitionSpec as P

NOPE = 128
ROPE = 64
LATENT = 512
VHEAD = 128
STEPS = 2

NZ, NX, NC = 4, 4, 2
NY, NL = 4, 2


def tensor_shift(value, dz=0, dx=0, dc=0):
    pairs = []
    for z in range(NZ):
        for x in range(NX):
            for c in range(NC):
                to = (((z + dz) % NZ) * NX + (x + dx) % NX) * NC + (c + dc) % NC
                pairs.append(((z * NX + x) * NC + c, to))
    return lax.ppermute(value, "tensor", pairs)


def dp_shift(value, dy=0, dl=0):
    pairs = []
    for y in range(NY):
        for l in range(NL):
            pairs.append((y * NL + l, ((y + dy) % NY) * NL + (l + dl) % NL))
    return lax.ppermute(value, "dp", pairs)


def wide_sum(parts):
    total = parts[0].astype(jnp.float32)
    for part in parts[1:]:
        total = total + part.astype(jnp.float32)
    return total


def gather_rows(value):
    value = jnp.stack([value] + [tensor_shift(value, dz=k) for k in range(1, NZ)])
    value = jnp.stack([value] + [tensor_shift(value, dx=k) for k in range(1, NX)])
    return jnp.stack([value, tensor_shift(value, dc=1)])


def scatter_sum(parts):
    mine = wide_sum([parts(0), tensor_shift(parts(1), dc=1)]).astype(jnp.bfloat16)
    mine = wide_sum(
        [mine[0]] + [tensor_shift(mine[k], dx=-k) for k in range(1, NX)]
    ).astype(jnp.bfloat16)
    return wide_sum([mine[0]] + [tensor_shift(mine[k], dz=-k) for k in range(1, NZ)])


def to_rows(value):
    value = jnp.stack([value[0], tensor_shift(value[1], dc=1)])
    value = jnp.stack([value[:, 0]] + [tensor_shift(value[:, k], dx=-k) for k in range(1, NX)])
    return jnp.stack(
        [value[:, :, 0]] + [tensor_shift(value[:, :, k], dz=-k) for k in range(1, NZ)]
    )


def to_heads(value):
    value = jnp.stack([value[0]] + [tensor_shift(value[k], dz=k) for k in range(1, NZ)])
    value = jnp.stack([value[:, 0]] + [tensor_shift(value[:, k], dx=k) for k in range(1, NX)])
    return jnp.stack([value[:, :, 0], tensor_shift(value[:, :, 1], dc=1)])


def rotate_pairs(pairs, position):
    half_width = pairs.shape[-1] // 2
    ladder = jnp.arange(half_width).astype(jnp.float32)
    frequency = jnp.exp(ladder * (-2.0 * math.log(10000.0) / pairs.shape[-1]))
    angle = position.astype(jnp.float32)[..., None] * frequency
    cosine = jnp.cos(angle)[..., None, :]
    sine_part = jnp.sin(angle)[..., None, :]
    first = pairs[..., :half_width].astype(jnp.float32)
    second = pairs[..., half_width:].astype(jnp.float32)
    return jnp.concatenate(
        [first * cosine - second * sine_part, first * sine_part + second * cosine], axis=-1
    )


def rms_scale(mixed, norm_gain):
    wide = mixed.astype(jnp.float32)
    factor = lax.rsqrt(jnp.mean(wide * wide, axis=-1, keepdims=True) + 1e-06)
    return (wide * factor * norm_gain.astype(jnp.float32)).astype(jnp.bfloat16)


def attend_rows(query, row_lengths, cache_rows, newest):
    scale = (NOPE + ROPE) ** (-0.5)
    slot_count = cache_rows.shape[1]
    scores = (
        jnp.einsum("rshc,rlc->rshl", query, cache_rows, preferred_element_type=jnp.float32) * scale
    )
    slots = jnp.arange(slot_count)
    scores = jnp.where(
        slots[None, None, None, :] < row_lengths[:, None, None, None], scores, -jnp.inf
    )
    own_scores = (
        jnp.einsum("rshc,rtc->rsht", query, newest, preferred_element_type=jnp.float32) * scale
    )
    steps = jnp.arange(STEPS)
    own_scores = jnp.where(
        steps[None, None, None, :] <= steps[None, :, None, None], own_scores, -jnp.inf
    )
    peak = jnp.maximum(
        jnp.max(scores, axis=-1, keepdims=True), jnp.max(own_scores, axis=-1, keepdims=True)
    )
    weights = jnp.exp(scores - peak)
    own_weights = jnp.exp(own_scores - peak)
    total = jnp.sum(weights, axis=-1, keepdims=True) + jnp.sum(own_weights, axis=-1, keepdims=True)
    probs = (weights / total).astype(jnp.bfloat16)
    own_probs = (own_weights / total).astype(jnp.bfloat16)
    gathered = jnp.einsum(
        "rshl,rlc->rshc", probs, cache_rows[..., :LATENT], preferred_element_type=jnp.float32
    )
    gathered = gathered + jnp.einsum(
        "rsht,rtc->rshc", own_probs, newest[..., :LATENT], preferred_element_type=jnp.float32
    )
    return gathered.astype(jnp.bfloat16)


def shards(
    query_latent,
    fresh_latent,
    stream,
    lengths,
    latent_cache,
    w_qb,
    w_uk,
    w_uv,
    w_o,
    norm_gain,
    w_gate,
    w_up,
    w_down,
):
    heads_here = w_uk.shape[0]
    rows_dev = lengths.shape[0]
    local = STEPS * rows_dev
    width = stream.shape[-1]
    chunk = w_gate.shape[0]
    units = w_gate.shape[1]
    dp_index = lax.axis_index("dp")
    y_index, l_index = dp_index // NL, dp_index % NL

    packed = jnp.concatenate([w_gate.T, w_up.T, w_down], axis=0)
    groups = [[y * NL + l for y in range(NY)] for l in range(NL)]
    weights = lax.all_gather(packed, "dp", axis=0, tiled=False, axis_index_groups=groups)

    pieces = []
    order = []
    for l in range(NL):
        base = dp_shift(w_qb, dl=1) if l else w_qb
        for y in range(NY):
            pieces.append(dp_shift(base, dy=y) if y else base)
            order.append((y_index - y) % NY * NL + (l_index + l) % NL)
    part = w_qb.shape[0]
    latent = query_latent.reshape(local, NY * NL, part)
    latent = jnp.take(latent, jnp.stack(order), axis=1).reshape(local, NY * NL * part)
    everyone = gather_rows(latent).reshape(-1, NY * NL * part)
    projected = jnp.dot(
        everyone, jnp.concatenate(pieces, axis=0), preferred_element_type=jnp.float32
    ).astype(jnp.bfloat16)
    projected = projected.reshape(-1, heads_here, NOPE + ROPE)
    absorbed = jnp.einsum(
        "nhd,hdc->nhc", projected[..., :NOPE], w_uk, preferred_element_type=jnp.float32
    ).astype(jnp.bfloat16)
    query = jnp.concatenate([absorbed, projected[..., NOPE:]], axis=2)
    query = query.reshape(NC, NX, NZ, local, heads_here * (LATENT + ROPE))

    query = to_rows(query).reshape(NZ * NX * NC, STEPS, rows_dev, heads_here, LATENT + ROPE)
    query = query.transpose(2, 1, 0, 3, 4).reshape(rows_dev, STEPS, -1, LATENT + ROPE)
    position = lengths[:, None] + jnp.arange(STEPS)[None, :]
    rotated = rotate_pairs(query[..., LATENT:], position).astype(jnp.bfloat16)
    query = jnp.concatenate([query[..., :LATENT], rotated], axis=-1)
    attended = attend_rows(query, lengths, latent_cache, jnp.swapaxes(fresh_latent, 0, 1))
    attended = attended.reshape(rows_dev, STEPS, NZ * NX * NC, heads_here, LATENT)
    attended = attended.transpose(2, 1, 0, 3, 4).reshape(
        NZ, NX, NC, local, heads_here * LATENT
    )
    returned = to_heads(attended).reshape(-1, heads_here, LATENT)
    head_values = jnp.einsum(
        "nhc,hcv->nhv", returned, w_uv, preferred_element_type=jnp.float32
    ).astype(jnp.bfloat16)
    head_values = head_values.reshape(-1, heads_here * VHEAD)
    terms = jnp.dot(head_values, w_o, preferred_element_type=jnp.float32).astype(jnp.bfloat16)
    terms = terms.reshape(NC, NX, NZ, local, width)
    attention_out = scatter_sum(lambda c: terms[c])
    mixed = (stream.reshape(local, width).astype(jnp.float32) + attention_out).astype(jnp.bfloat16)
    normed = rms_scale(mixed, norm_gain)

    split = normed.reshape(local, NY, NL, chunk)
    kept = lax.dynamic_index_in_dim(split, l_index, axis=2, keepdims=False)
    sent = lax.dynamic_index_in_dim(split, 1 - l_index, axis=2, keepdims=False)
    pair = jnp.stack([kept, dp_shift(sent, dl=1)])
    everyone = gather_rows(pair).reshape(-1, NY, chunk)
    both = jnp.zeros((everyone.shape[0], 2 * units), jnp.float32)
    for y in range(NY):
        both = both + lax.dot_general(
            everyone[:, y],
            weights[y, : 2 * units],
            (((1,), (1,)), ((), ())),
            preferred_element_type=jnp.float32,
        )
    both = both.reshape(NC * NX * NZ, 2, local, 2 * units)
    away = dp_shift(both[:, 1].astype(jnp.bfloat16), dl=1)
    both = both[:, 0] + away.astype(jnp.float32)
    hidden = (jax.nn.silu(both[..., :units]) * both[..., units:]).astype(jnp.bfloat16)
    hidden = jnp.stack([hidden, dp_shift(hidden, dl=1)], axis=1).reshape(-1, units)
    terms = jnp.stack(
        [
            jnp.dot(hidden, weights[y, 2 * units :], preferred_element_type=jnp.float32).astype(
                jnp.bfloat16
            )
            for y in range(NY)
        ],
        axis=1,
    )
    terms = terms.reshape(NC, NX, NZ, 2, local, NY, chunk)
    value = scatter_sum(lambda c: terms[c])
    away = dp_shift(value[1].astype(jnp.bfloat16), dl=1).astype(jnp.float32)
    value = jnp.stack(
        [jnp.where(l_index == 0, value[0], away), jnp.where(l_index == 0, away, value[0])], axis=2
    ).reshape(local, width)
    out = (mixed.astype(jnp.float32) + value).astype(jnp.bfloat16)
    return out.reshape(STEPS, rows_dev, width)


def solution(mesh):
    placed = (
        P(None, ("dp", "tensor"), None),
        P(None, ("dp", "tensor"), None),
        P(None, ("dp", "tensor"), None),
        P(("dp", "tensor")),
        P(("dp", "tensor"), None, None),
        P("dp", "tensor"),
        P("tensor", None, None),
        P("tensor", None, None),
        P("tensor", None),
        P(),
        P("dp", "tensor"),
        P("dp", "tensor"),
        P("tensor", "dp"),
    )
    return jax.shard_map(
        shards,
        mesh=mesh,
        in_specs=placed,
        out_specs=P(None, ("dp", "tensor"), None),
        check_vma=False,
    )
```

```python
import math

import jax
import jax.numpy as jnp
from jax import lax
from jax.sharding import Mesh, PartitionSpec as P

NOPE = 128
ROPE = 64
LATENT = 512
VHEAD = 128
STEPS = 2

SIZES = {"y": 4, "l": 2, "z": 4, "x": 4, "c": 2}
DP = ("y", "l")
TENSOR = ("z", "x", "c")
HEADS = ("c", "x", "z")


def shift(value, axis, by):
    size = SIZES[axis]
    return lax.ppermute(value, axis, [(i, (i + by) % size) for i in range(size)])


def gather_back(value, axis):
    return jnp.concatenate(
        [value] + [shift(value, axis, k) for k in range(1, SIZES[axis])], axis=0
    )


def scatter_back(parts, axis):
    total = parts[0].astype(jnp.float32)
    for k in range(1, SIZES[axis]):
        total = total + shift(parts[k], axis, -k).astype(jnp.float32)
    return total


def scatter_rows(terms):
    for axis in ("x", "z"):
        rows = terms.shape[0] // SIZES[axis]
        parts = [terms[k * rows : (k + 1) * rows] for k in range(SIZES[axis])]
        terms = scatter_back(parts, axis)
        if axis == "x":
            terms = terms.astype(jnp.bfloat16)
    return terms


def rotate_pairs(pairs, position):
    half_width = pairs.shape[-1] // 2
    ladder = jnp.arange(half_width).astype(jnp.float32)
    frequency = jnp.exp(ladder * (-2.0 * math.log(10000.0) / pairs.shape[-1]))
    angle = position.astype(jnp.float32)[..., None] * frequency
    cosine = jnp.cos(angle)[..., None, :]
    sine_part = jnp.sin(angle)[..., None, :]
    first = pairs[..., :half_width].astype(jnp.float32)
    second = pairs[..., half_width:].astype(jnp.float32)
    return jnp.concatenate(
        [first * cosine - second * sine_part, first * sine_part + second * cosine], axis=-1
    )


def rms_scale(mixed, norm_gain):
    wide = mixed.astype(jnp.float32)
    factor = lax.rsqrt(jnp.mean(wide * wide, axis=-1, keepdims=True) + 1e-06)
    return (wide * factor * norm_gain.astype(jnp.float32)).astype(jnp.bfloat16)


def attend_rows(query, row_lengths, cache_rows, newest):
    scale = (NOPE + ROPE) ** (-0.5)
    slot_count = cache_rows.shape[1]
    scores = (
        jnp.einsum("rshc,rlc->rshl", query, cache_rows, preferred_element_type=jnp.float32) * scale
    )
    slots = jnp.arange(slot_count)
    scores = jnp.where(
        slots[None, None, None, :] < row_lengths[:, None, None, None], scores, -jnp.inf
    )
    own_scores = (
        jnp.einsum("rshc,rtc->rsht", query, newest, preferred_element_type=jnp.float32) * scale
    )
    steps = jnp.arange(STEPS)
    own_scores = jnp.where(
        steps[None, None, None, :] <= steps[None, :, None, None], own_scores, -jnp.inf
    )
    peak = jnp.maximum(
        jnp.max(scores, axis=-1, keepdims=True), jnp.max(own_scores, axis=-1, keepdims=True)
    )
    weights = jnp.exp(scores - peak)
    own_weights = jnp.exp(own_scores - peak)
    total = jnp.sum(weights, axis=-1, keepdims=True) + jnp.sum(own_weights, axis=-1, keepdims=True)
    probs = (weights / total).astype(jnp.bfloat16)
    own_probs = (own_weights / total).astype(jnp.bfloat16)
    gathered = jnp.einsum(
        "rshl,rlc->rshc", probs, cache_rows[..., :LATENT], preferred_element_type=jnp.float32
    )
    gathered = gathered + jnp.einsum(
        "rsht,rtc->rshc", own_probs, newest[..., :LATENT], preferred_element_type=jnp.float32
    )
    return gathered.astype(jnp.bfloat16)


def shards(
    query_latent,
    fresh_latent,
    stream,
    lengths,
    latent_cache,
    w_qb,
    w_uk,
    w_uv,
    w_o,
    norm_gain,
    w_gate,
    w_up,
    w_down,
):
    bf16 = jnp.bfloat16
    heads_here = w_uk.shape[0]
    rows_dev = lengths.shape[0]
    local = STEPS * rows_dev
    width = stream.shape[-1]
    chunk, units = w_gate.shape
    part = w_qb.shape[0]
    ny, nl, nz, nx, nc = (SIZES[a] for a in ("y", "l", "z", "x", "c"))
    here = {axis: lax.axis_index(axis) for axis in SIZES}
    l_index = here["l"]
    turned = jnp.stack(
        [
            ((here["c"] - c) % nc * nx + (here["x"] - x) % nx) * nz + (here["z"] - z) % nz
            for c in range(nc)
            for x in range(nx)
            for z in range(nz)
        ]
    )

    def by_pair(kept, sent):
        sent = shift(sent, "l", 1)
        return jnp.where(l_index == 0, kept, sent), jnp.where(l_index == 0, sent, kept)

    query_weights = lax.all_gather(w_qb, "y", axis=0, tiled=True)
    split = query_latent.reshape(local, ny, nl, part)
    kept = lax.dynamic_index_in_dim(split, l_index, axis=2, keepdims=False)
    sent = lax.dynamic_index_in_dim(split, 1 - l_index, axis=2, keepdims=False)
    pair = by_pair(kept.reshape(local, ny * part), sent.reshape(local, ny * part))
    packed = jnp.concatenate([w_gate.T, w_up.T, w_down], axis=0)
    pair, packed = lax.optimization_barrier((jnp.concatenate(pair, axis=0), packed))
    weights = lax.all_gather(packed, "y", axis=1, tiled=True)
    everyone = gather_back(gather_back(gather_back(pair, "z"), "x"), "c")

    projected = jnp.dot(everyone, query_weights, preferred_element_type=jnp.float32)
    projected = projected.reshape(nc * nx * nz, nl, local, projected.shape[-1])
    kept = jnp.where(l_index == 0, projected[:, 0], projected[:, 1])
    sent = jnp.where(l_index == 0, projected[:, 1], projected[:, 0]).astype(bf16)
    projected = kept + shift(sent, "l", 1).astype(jnp.float32)
    projected = projected.astype(bf16).reshape(-1, heads_here, NOPE + ROPE)
    absorbed = jnp.einsum(
        "nhd,hdc->nhc", projected[..., :NOPE], w_uk, preferred_element_type=jnp.float32
    ).astype(bf16)
    query = jnp.concatenate([absorbed, projected[..., NOPE:]], axis=2)
    query = query.reshape(nc * nx * nz, local, heads_here * (LATENT + ROPE))
    query = lax.all_to_all(jnp.take(query, turned, axis=0), HEADS, 0, 0, tiled=True)

    query = query.reshape(-1, STEPS, rows_dev, heads_here, LATENT + ROPE)
    query = query.transpose(2, 1, 0, 3, 4).reshape(rows_dev, STEPS, -1, LATENT + ROPE)
    position = lengths[:, None] + jnp.arange(STEPS)[None, :]
    rotated = rotate_pairs(query[..., LATENT:], position).astype(bf16)
    query = jnp.concatenate([query[..., :LATENT], rotated], axis=-1)
    attended = attend_rows(query, lengths, latent_cache, jnp.swapaxes(fresh_latent, 0, 1))
    attended = attended.reshape(rows_dev, STEPS, -1, heads_here, LATENT)
    attended = attended.transpose(2, 1, 0, 3, 4).reshape(-1, local, heads_here * LATENT)

    returned = lax.all_to_all(attended, HEADS, 0, 0, tiled=True)
    returned = returned.reshape(-1, heads_here, LATENT)
    head_values = jnp.einsum(
        "nhc,hcv->nhv", returned, w_uv, preferred_element_type=jnp.float32
    ).astype(bf16)
    head_values = head_values.reshape(nc * nx * nz, local * heads_here * VHEAD)
    head_values = jnp.take(head_values, turned, axis=0).reshape(-1, heads_here * VHEAD)
    head_values, weights = lax.optimization_barrier((head_values, weights))
    terms = jnp.dot(head_values, w_o, preferred_element_type=jnp.float32).astype(bf16)
    half = terms.shape[0] // 2
    terms = terms[:half].astype(jnp.float32) + shift(terms[half:], "c", 1).astype(jnp.float32)
    attention_out = scatter_rows(terms.astype(bf16))
    mixed = (stream.reshape(local, width).astype(jnp.float32) + attention_out).astype(bf16)
    normed = rms_scale(mixed, norm_gain)

    split = normed.reshape(local, ny, nl, chunk)
    kept = lax.dynamic_index_in_dim(split, l_index, axis=2, keepdims=False)
    sent = lax.dynamic_index_in_dim(split, 1 - l_index, axis=2, keepdims=False)
    pair = by_pair(kept.reshape(local, ny * chunk), sent.reshape(local, ny * chunk))
    first = gather_back(gather_back(jnp.concatenate(pair, axis=0), "z"), "x")
    second = shift(first, "c", 1)

    def gate_up(rows):
        return lax.dot_general(
            rows,
            weights[: 2 * units],
            (((1,), (1,)), ((), ())),
            preferred_element_type=jnp.float32,
        )

    def down(both, away):
        both = both + away.astype(jnp.float32)
        hidden = (jax.nn.silu(both[:, :units]) * both[:, units:]).astype(bf16)
        return jnp.dot(hidden, weights[2 * units :], preferred_element_type=jnp.float32)

    first, second = gate_up(first), gate_up(second)
    first_away = shift(first.astype(bf16), "l", 1)
    second_away = shift(second.astype(bf16), "l", 1)
    away = shift(down(second, second_away).astype(bf16), "c", 1)
    terms = down(first, first_away) + away.astype(jnp.float32)
    value = scatter_rows(terms.astype(bf16))
    sent = jnp.where(l_index == 0, value[local:], value[:local]).astype(bf16)
    value = jnp.where(l_index == 0, value[:local], value[local:])
    sent = shift(sent, "l", 1).astype(jnp.float32)
    value = jnp.stack(
        [
            jnp.where(l_index == 0, value, sent).reshape(local, ny, chunk),
            jnp.where(l_index == 0, sent, value).reshape(local, ny, chunk),
        ],
        axis=2,
    ).reshape(local, width)
    out = (mixed.astype(jnp.float32) + value).astype(bf16)
    return out.reshape(STEPS, rows_dev, width)


def solution(mesh):
    parts = Mesh(mesh.devices.reshape(tuple(SIZES.values())), tuple(SIZES))
    rows = P(None, DP + TENSOR, None)
    placed = (
        rows,
        rows,
        rows,
        P(DP + TENSOR),
        P(DP + TENSOR, None, None),
        P(DP, TENSOR),
        P(TENSOR, None, None),
        P(TENSOR, None, None),
        P(TENSOR, None),
        P(),
        P(DP, TENSOR),
        P(DP, TENSOR),
        P(TENSOR, DP),
    )
    return jax.shard_map(
        shards, mesh=parts, in_specs=placed, out_specs=rows, check_vma=False
    )
```

```python
import math

import jax
import jax.numpy as jnp
from jax import lax
from jax.sharding import Mesh, PartitionSpec as P

NOPE = 128
ROPE = 64
LATENT = 512
VHEAD = 128
STEPS = 2

SIZES = {"y": 4, "l": 2, "z": 4, "x": 4, "c": 2}
DP = ("y", "l")
TENSOR = ("z", "x", "c")
HEADS = ("c", "x", "z")


def shift(value, axis, by):
    size = SIZES[axis]
    return lax.ppermute(value, axis, [(i, (i + by) % size) for i in range(size)])


def gather_back(value, axis):
    return jnp.concatenate(
        [value] + [shift(value, axis, k) for k in range(1, SIZES[axis])], axis=0
    )


def scatter_back(parts, axis):
    total = parts[0].astype(jnp.float32)
    for k in range(1, SIZES[axis]):
        total = total + shift(parts[k], axis, -k).astype(jnp.float32)
    return total


def scatter_rows(terms):
    for axis in ("x", "z"):
        rows = terms.shape[0] // SIZES[axis]
        parts = [terms[k * rows : (k + 1) * rows] for k in range(SIZES[axis])]
        terms = scatter_back(parts, axis)
        if axis == "x":
            terms = terms.astype(jnp.bfloat16)
    return terms


def rotate_pairs(pairs, position):
    half_width = pairs.shape[-1] // 2
    ladder = jnp.arange(half_width).astype(jnp.float32)
    frequency = jnp.exp(ladder * (-2.0 * math.log(10000.0) / pairs.shape[-1]))
    angle = position.astype(jnp.float32)[..., None] * frequency
    cosine = jnp.cos(angle)[..., None, :]
    sine_part = jnp.sin(angle)[..., None, :]
    first = pairs[..., :half_width].astype(jnp.float32)
    second = pairs[..., half_width:].astype(jnp.float32)
    return jnp.concatenate(
        [first * cosine - second * sine_part, first * sine_part + second * cosine], axis=-1
    )


def rms_scale(mixed, norm_gain):
    wide = mixed.astype(jnp.float32)
    factor = lax.rsqrt(jnp.mean(wide * wide, axis=-1, keepdims=True) + 1e-06)
    return (wide * factor * norm_gain.astype(jnp.float32)).astype(jnp.bfloat16)


def attend_rows(query, row_lengths, cache_rows, newest):
    scale = (NOPE + ROPE) ** (-0.5)
    slot_count = cache_rows.shape[1]
    scores = (
        jnp.einsum("rshc,rlc->rshl", query, cache_rows, preferred_element_type=jnp.float32) * scale
    )
    slots = jnp.arange(slot_count)
    scores = jnp.where(
        slots[None, None, None, :] < row_lengths[:, None, None, None], scores, -jnp.inf
    )
    own_scores = (
        jnp.einsum("rshc,rtc->rsht", query, newest, preferred_element_type=jnp.float32) * scale
    )
    steps = jnp.arange(STEPS)
    own_scores = jnp.where(
        steps[None, None, None, :] <= steps[None, :, None, None], own_scores, -jnp.inf
    )
    peak = jnp.maximum(
        jnp.max(scores, axis=-1, keepdims=True), jnp.max(own_scores, axis=-1, keepdims=True)
    )
    weights = jnp.exp(scores - peak)
    own_weights = jnp.exp(own_scores - peak)
    total = jnp.sum(weights, axis=-1, keepdims=True) + jnp.sum(own_weights, axis=-1, keepdims=True)
    probs = (weights / total).astype(jnp.bfloat16)
    own_probs = (own_weights / total).astype(jnp.bfloat16)
    gathered = jnp.einsum(
        "rshl,rlc->rshc", probs, cache_rows[..., :LATENT], preferred_element_type=jnp.float32
    )
    gathered = gathered + jnp.einsum(
        "rsht,rtc->rshc", own_probs, newest[..., :LATENT], preferred_element_type=jnp.float32
    )
    return gathered.astype(jnp.bfloat16)


def shards(
    query_latent,
    fresh_latent,
    stream,
    lengths,
    latent_cache,
    w_qb,
    w_uk,
    w_uv,
    w_o,
    norm_gain,
    w_gate,
    w_up,
    w_down,
):
    bf16 = jnp.bfloat16
    heads_here = w_uk.shape[0]
    rows_dev = lengths.shape[0]
    local = STEPS * rows_dev
    width = stream.shape[-1]
    chunk, units = w_gate.shape
    part = w_qb.shape[0]
    ny, nl, nz, nx, nc = (SIZES[a] for a in ("y", "l", "z", "x", "c"))
    here = {axis: lax.axis_index(axis) for axis in SIZES}
    l_index = here["l"]
    turned = jnp.stack(
        [
            ((here["c"] - c) % nc * nx + (here["x"] - x) % nx) * nz + (here["z"] - z) % nz
            for c in range(nc)
            for x in range(nx)
            for z in range(nz)
        ]
    )

    def by_pair(kept, sent):
        sent = shift(sent, "l", 1)
        return jnp.where(l_index == 0, kept, sent), jnp.where(l_index == 0, sent, kept)

    query_weights = lax.all_gather(w_qb, "y", axis=0, tiled=True)
    split = query_latent.reshape(local, ny, nl, part)
    kept = lax.dynamic_index_in_dim(split, l_index, axis=2, keepdims=False)
    sent = lax.dynamic_index_in_dim(split, 1 - l_index, axis=2, keepdims=False)
    pair = by_pair(kept.reshape(local, ny * part), sent.reshape(local, ny * part))
    everyone = gather_back(jnp.concatenate(pair, axis=0), "z")

    packed = jnp.concatenate([w_gate.T, w_up.T, w_down], axis=0)
    everyone, packed = lax.optimization_barrier((everyone, packed))
    weights = lax.all_gather(packed, "y", axis=1, tiled=True)
    everyone = gather_back(gather_back(everyone, "x"), "c")

    projected = jnp.dot(everyone, query_weights, preferred_element_type=jnp.float32)
    projected = projected.reshape(nc * nx * nz, nl, local, projected.shape[-1])
    kept = jnp.where(l_index == 0, projected[:, 0], projected[:, 1])
    sent = jnp.where(l_index == 0, projected[:, 1], projected[:, 0]).astype(bf16)
    projected = kept + shift(sent, "l", 1).astype(jnp.float32)
    projected = projected.astype(bf16).reshape(-1, heads_here, NOPE + ROPE)
    absorbed = jnp.einsum(
        "nhd,hdc->nhc", projected[..., :NOPE], w_uk, preferred_element_type=jnp.float32
    ).astype(bf16)
    query = jnp.concatenate([absorbed, projected[..., NOPE:]], axis=2)
    query = query.reshape(nc * nx * nz, local, heads_here * (LATENT + ROPE))
    query = lax.all_to_all(jnp.take(query, turned, axis=0), HEADS, 0, 0, tiled=True)

    query = query.reshape(-1, STEPS, rows_dev, heads_here, LATENT + ROPE)
    query = query.transpose(2, 1, 0, 3, 4).reshape(rows_dev, STEPS, -1, LATENT + ROPE)
    position = lengths[:, None] + jnp.arange(STEPS)[None, :]
    rotated = rotate_pairs(query[..., LATENT:], position).astype(bf16)
    query = jnp.concatenate([query[..., :LATENT], rotated], axis=-1)
    attended = attend_rows(query, lengths, latent_cache, jnp.swapaxes(fresh_latent, 0, 1))
    attended = attended.reshape(rows_dev, STEPS, -1, heads_here, LATENT)
    attended = attended.transpose(2, 1, 0, 3, 4).reshape(-1, local, heads_here * LATENT)

    returned = lax.all_to_all(attended, HEADS, 0, 0, tiled=True)
    returned = returned.reshape(-1, heads_here, LATENT)
    head_values = jnp.einsum(
        "nhc,hcv->nhv", returned, w_uv, preferred_element_type=jnp.float32
    ).astype(bf16)
    head_values = head_values.reshape(nc * nx * nz, local * heads_here * VHEAD)
    head_values = jnp.take(head_values, turned, axis=0).reshape(-1, heads_here * VHEAD)
    head_values, weights = lax.optimization_barrier((head_values, weights))
    terms = jnp.dot(head_values, w_o, preferred_element_type=jnp.float32).astype(bf16)
    half = terms.shape[0] // 2
    terms = terms[:half].astype(jnp.float32) + shift(terms[half:], "c", 1).astype(jnp.float32)
    attention_out = scatter_rows(terms.astype(bf16))
    mixed = (stream.reshape(local, width).astype(jnp.float32) + attention_out).astype(bf16)
    normed = rms_scale(mixed, norm_gain)

    split = normed.reshape(local, ny, nl, chunk)
    kept = lax.dynamic_index_in_dim(split, l_index, axis=2, keepdims=False)
    sent = lax.dynamic_index_in_dim(split, 1 - l_index, axis=2, keepdims=False)
    pair = by_pair(kept.reshape(local, ny * chunk), sent.reshape(local, ny * chunk))
    first = lax.optimization_barrier(gather_back(jnp.concatenate(pair, axis=0), "z"))
    first = lax.optimization_barrier(gather_back(first, "x"))
    second = shift(first, "c", 1)

    def gate_up(rows):
        return lax.dot_general(
            rows,
            weights[: 2 * units],
            (((1,), (1,)), ((), ())),
            preferred_element_type=jnp.float32,
        )

    def down(both, away):
        both = both + away.astype(jnp.float32)
        hidden = (jax.nn.silu(both[:, :units]) * both[:, units:]).astype(bf16)
        return jnp.dot(hidden, weights[2 * units :], preferred_element_type=jnp.float32)

    first, second = gate_up(first), gate_up(second)
    first_away = shift(first.astype(bf16), "l", 1)
    second_away = shift(second.astype(bf16), "l", 1)
    first_away, second_away = lax.optimization_barrier((first_away, second_away))
    away = shift(down(second, second_away).astype(bf16), "c", 1)
    terms = down(first, first_away) + away.astype(jnp.float32)
    value = scatter_rows(terms.astype(bf16))
    sent = jnp.where(l_index == 0, value[local:], value[:local]).astype(bf16)
    value = jnp.where(l_index == 0, value[:local], value[local:])
    sent = shift(sent, "l", 1).astype(jnp.float32)
    value = jnp.stack(
        [
            jnp.where(l_index == 0, value, sent).reshape(local, ny, chunk),
            jnp.where(l_index == 0, sent, value).reshape(local, ny, chunk),
        ],
        axis=2,
    ).reshape(local, width)
    out = (mixed.astype(jnp.float32) + value).astype(bf16)
    return out.reshape(STEPS, rows_dev, width)


def solution(mesh):
    parts = Mesh(mesh.devices.reshape(tuple(SIZES.values())), tuple(SIZES))
    rows = P(None, DP + TENSOR, None)
    placed = (
        rows,
        rows,
        rows,
        P(DP + TENSOR),
        P(DP + TENSOR, None, None),
        P(DP, TENSOR),
        P(TENSOR, None, None),
        P(TENSOR, None, None),
        P(TENSOR, None),
        P(),
        P(DP, TENSOR),
        P(DP, TENSOR),
        P(TENSOR, DP),
    )
    return jax.shard_map(
        shards, mesh=parts, in_specs=placed, out_specs=rows, check_vma=False
    )
```

```python
import math

import jax
import jax.numpy as jnp
from jax import lax
from jax.experimental import pallas as pl
from jax.experimental.pallas import tpu as pltpu
from jax.sharding import Mesh, PartitionSpec as P

NOPE = 128
ROPE = 64
LATENT = 512
VHEAD = 128
STEPS = 2

SIZES = {"y": 4, "l": 2, "z": 4, "x": 4, "c": 2}
DP = ("y", "l")
TENSOR = ("z", "x", "c")
HEADS = ("c", "x", "z")


def shift(value, axis, by):
    size = SIZES[axis]
    return lax.ppermute(value, axis, [(i, (i + by) % size) for i in range(size)])


def nearest_first(size):
    return sorted(range(1, size), key=lambda k: min(k, size - k))


def gather_back(value, axis):
    parts = {0: value}
    for k in nearest_first(SIZES[axis]):
        parts[k] = shift(value, axis, k)
    return jnp.concatenate([parts[k] for k in range(SIZES[axis])], axis=0)


def scatter_back(parts, axis):
    total = parts[0].astype(jnp.float32)
    for by in nearest_first(SIZES[axis]):
        part = parts[SIZES[axis] - by]
        total = total + shift(part, axis, by).astype(jnp.float32)
    return total


def scatter_rows(terms):
    for axis in ("x", "z"):
        rows = terms.shape[0] // SIZES[axis]
        parts = [terms[k * rows : (k + 1) * rows] for k in range(SIZES[axis])]
        terms = scatter_back(parts, axis)
        if axis == "x":
            terms = terms.astype(jnp.bfloat16)
    return terms


def rms_scale(mixed, norm_gain):
    wide = mixed.astype(jnp.float32)
    factor = lax.rsqrt(jnp.mean(wide * wide, axis=-1, keepdims=True) + 1e-06)
    return (wide * factor * norm_gain.astype(jnp.float32)).astype(jnp.bfloat16)


def attend_rows(query, keys, lengths, turn):
    steps, rows, places, wide = query.shape
    heads = wide // (LATENT + ROPE)
    slots = keys.shape[2] - 128
    scale = (NOPE + ROPE) ** (-0.5)
    per_step = heads * places

    def body(lengths_ref, query_ref, keys_ref, turn_ref, out_ref):
        row = pl.program_id(0)
        content, rotary = [], []
        lane = lax.broadcasted_iota(jnp.int32, (places, 2 * ROPE), 1)
        first_half = lane % ROPE < ROPE // 2
        for step in range(steps):
            for head in range(heads):
                content.append(query_ref[step, 0, :, head * LATENT : (head + 1) * LATENT])
            for pair in range(heads // 2):
                at = heads * LATENT + pair * 2 * ROPE
                value = query_ref[step, 0, :, at : at + 2 * ROPE].astype(jnp.float32)
                other = jnp.where(
                    first_half,
                    pltpu.roll(value, 2 * ROPE - ROPE // 2, 1),
                    pltpu.roll(value, ROPE // 2, 1),
                )
                cosine = turn_ref[0, step, pl.ds(row, 1)]
                sine_part = turn_ref[1, step, pl.ds(row, 1)]
                value = value * cosine + other * sine_part
                rotary.append(jnp.where(lane < ROPE, value, 0.0).astype(jnp.bfloat16))
                rotary.append(jnp.where(lane < ROPE, 0.0, value).astype(jnp.bfloat16))
        content = jnp.concatenate(content, axis=0)
        rotary = jnp.concatenate(rotary, axis=0)
        latents = keys_ref[0, :LATENT]
        turned = keys_ref[0, LATENT:]
        scores = jnp.dot(content, latents, preferred_element_type=jnp.float32)
        scores += jnp.dot(
            rotary, jnp.concatenate([turned, turned], axis=0), preferred_element_type=jnp.float32
        )
        slot = lax.broadcasted_iota(jnp.int32, scores.shape, 1)
        step = lax.broadcasted_iota(jnp.int32, scores.shape, 0) // per_step
        fresh = slot - slots
        seen = (slot < lengths_ref[row]) | ((fresh >= 0) & (fresh <= step))
        scores = jnp.where(seen, scores * scale, -jnp.inf)
        weights = jnp.exp(scores - jnp.max(scores, axis=1, keepdims=True))
        probs = weights / jnp.sum(weights, axis=1, keepdims=True)
        out = lax.dot_general(
            probs.astype(jnp.bfloat16),
            latents,
            (((1,), (1,)), ((), ())),
            preferred_element_type=jnp.float32,
        ).astype(jnp.bfloat16)
        for step in range(steps):
            for head in range(heads):
                at = step * per_step + head * places
                out_ref[step, 0, :, head * LATENT : (head + 1) * LATENT] = out[at : at + places]

    return pl.pallas_call(
        body,
        grid_spec=pltpu.PrefetchScalarGridSpec(
            num_scalar_prefetch=1,
            grid=(rows,),
            in_specs=[
                pl.BlockSpec((steps, 1, places, wide), lambda r, _: (0, r, 0, 0)),
                pl.BlockSpec((1,) + keys.shape[1:], lambda r, _: (r, 0, 0)),
                pl.BlockSpec(turn.shape, lambda r, _: (0, 0, 0, 0)),
            ],
            out_specs=pl.BlockSpec((steps, 1, places, heads * LATENT), lambda r, _: (0, r, 0, 0)),
        ),
        out_shape=jax.ShapeDtypeStruct((steps, rows, places, heads * LATENT), jnp.bfloat16),
        cost_estimate=pl.CostEstimate(
            flops=4 * rows * steps * per_step * LATENT * slots,
            bytes_accessed=4 * query.size + 2 * keys.size,
            transcendentals=rows * steps * per_step * slots,
        ),
        compiler_params=pltpu.CompilerParams(vmem_limit_bytes=32 * 1024 * 1024),
    )(lengths, query, keys, turn)


def shards(
    query_latent,
    fresh_latent,
    stream,
    lengths,
    latent_cache,
    w_qb,
    w_uk,
    w_uv,
    w_o,
    norm_gain,
    w_gate,
    w_up,
    w_down,
):
    bf16 = jnp.bfloat16
    heads_here = w_uk.shape[0]
    rows_dev = lengths.shape[0]
    local = STEPS * rows_dev
    width = stream.shape[-1]
    chunk, units = w_gate.shape
    part = w_qb.shape[0]
    ny, nl, nz, nx, nc = (SIZES[a] for a in ("y", "l", "z", "x", "c"))
    here = {axis: lax.axis_index(axis) for axis in SIZES}
    l_index = here["l"]
    turned = jnp.stack(
        [
            ((here["c"] - c) % nc * nx + (here["x"] - x) % nx) * nz + (here["z"] - z) % nz
            for c in range(nc)
            for x in range(nx)
            for z in range(nz)
        ]
    )

    def by_pair(kept, sent):
        sent = shift(sent, "l", 1)
        return jnp.where(l_index == 0, kept, sent), jnp.where(l_index == 0, sent, kept)

    query_weights = lax.all_gather(w_qb, "y", axis=0, tiled=True)
    split = query_latent.reshape(local, ny, nl, part)
    kept = lax.dynamic_index_in_dim(split, l_index, axis=2, keepdims=False)
    sent = lax.dynamic_index_in_dim(split, 1 - l_index, axis=2, keepdims=False)
    pair = by_pair(kept.reshape(local, ny * part), sent.reshape(local, ny * part))
    everyone = gather_back(jnp.concatenate(pair, axis=0), "z")

    packed = jnp.concatenate([w_gate.T, w_up.T, w_down], axis=0)
    everyone, packed = lax.optimization_barrier((everyone, packed))
    weights = lax.all_gather(packed, "y", axis=1, tiled=True)
    everyone = gather_back(gather_back(everyone, "x"), "c")

    projected = jnp.dot(everyone, query_weights, preferred_element_type=jnp.float32)
    projected = projected.reshape(nc * nx * nz, nl, local, projected.shape[-1])
    kept = jnp.where(l_index == 0, projected[:, 0], projected[:, 1])
    sent = jnp.where(l_index == 0, projected[:, 1], projected[:, 0]).astype(bf16)
    projected = kept + shift(sent, "l", 1).astype(jnp.float32)
    projected = projected.astype(bf16).reshape(-1, heads_here, NOPE + ROPE)
    absorbed = jnp.einsum(
        "nhd,hdc->nhc", projected[..., :NOPE], w_uk, preferred_element_type=jnp.float32
    ).astype(bf16)
    query = jnp.concatenate(
        [
            absorbed.reshape(-1, heads_here * LATENT),
            projected[..., NOPE:].reshape(-1, heads_here * ROPE),
        ],
        axis=1,
    )
    query = query.reshape(nc * nx * nz, local, heads_here * (LATENT + ROPE))
    query = lax.all_to_all(jnp.take(query, turned, axis=0, mode="clip"), HEADS, 0, 0, tiled=True)

    fresh = jnp.transpose(fresh_latent, (1, 2, 0))
    keys = jnp.concatenate(
        [
            jnp.swapaxes(latent_cache, 1, 2),
            jnp.pad(fresh, ((0, 0), (0, 0), (0, 128 - STEPS))),
        ],
        axis=2,
    )
    ladder = jnp.arange(ROPE // 2).astype(jnp.float32)
    frequency = jnp.exp(ladder * (-2.0 * math.log(10000.0) / ROPE))
    position = (lengths[None, :] + jnp.arange(STEPS)[:, None]).astype(jnp.float32)
    angle = position[:, :, None] * frequency
    cosine, sine_part = jnp.cos(angle), jnp.sin(angle)
    turn = jnp.stack(
        [
            jnp.concatenate([cosine, cosine, cosine, cosine], axis=-1),
            jnp.concatenate([-sine_part, sine_part, -sine_part, sine_part], axis=-1),
        ]
    )
    query, keys, turn = lax.optimization_barrier((query, keys, turn))
    query = query.reshape(-1, STEPS, rows_dev, query.shape[-1]).transpose(1, 2, 0, 3)
    attended = attend_rows(query, keys, lengths, turn)
    attended = attended.transpose(2, 0, 1, 3).reshape(-1, local, heads_here * LATENT)

    returned = lax.all_to_all(attended, HEADS, 0, 0, tiled=True)
    returned = returned.reshape(-1, heads_here, LATENT)
    head_values = jnp.einsum(
        "nhc,hcv->nhv", returned, w_uv, preferred_element_type=jnp.float32
    ).astype(bf16)
    head_values = head_values.reshape(nc * nx * nz, local * heads_here * VHEAD)
    head_values = jnp.take(head_values, turned, axis=0, mode="clip").reshape(-1, heads_here * VHEAD)
    terms = jnp.dot(head_values, w_o, preferred_element_type=jnp.float32).astype(bf16)
    terms, weights = lax.optimization_barrier((terms, weights))
    half = terms.shape[0] // 2
    terms = terms[:half].astype(jnp.float32) + shift(terms[half:], "c", 1).astype(jnp.float32)
    attention_out = scatter_rows(terms.astype(bf16))
    mixed = (stream.reshape(local, width).astype(jnp.float32) + attention_out).astype(bf16)
    normed = rms_scale(mixed, norm_gain)

    split = normed.reshape(local, ny, nl, chunk)
    kept = lax.dynamic_index_in_dim(split, l_index, axis=2, keepdims=False)
    sent = lax.dynamic_index_in_dim(split, 1 - l_index, axis=2, keepdims=False)
    pair = by_pair(kept.reshape(local, ny * chunk), sent.reshape(local, ny * chunk))
    first = lax.optimization_barrier(gather_back(jnp.concatenate(pair, axis=0), "z"))
    first = lax.optimization_barrier(gather_back(first, "x"))
    second = shift(first, "c", 1)

    def gate_up(rows):
        return lax.dot_general(
            rows,
            weights[: 2 * units],
            (((1,), (1,)), ((), ())),
            preferred_element_type=jnp.float32,
        )

    def down(both, away):
        both = both + away.astype(jnp.float32)
        hidden = (jax.nn.silu(both[:, :units]) * both[:, units:]).astype(bf16)
        return jnp.dot(hidden, weights[2 * units :], preferred_element_type=jnp.float32)

    first, second = gate_up(first), gate_up(second)
    first_away = shift(first.astype(bf16), "l", 1)
    second_away = shift(second.astype(bf16), "l", 1)
    first_away, second_away = lax.optimization_barrier((first_away, second_away))
    away = shift(down(second, second_away).astype(bf16), "c", 1)
    terms = down(first, first_away) + away.astype(jnp.float32)
    value = scatter_rows(terms.astype(bf16))
    sent = jnp.where(l_index == 0, value[local:], value[:local]).astype(bf16)
    value = jnp.where(l_index == 0, value[:local], value[local:])
    sent = shift(sent, "l", 1).astype(jnp.float32)
    value = jnp.stack(
        [
            jnp.where(l_index == 0, value, sent).reshape(local, ny, chunk),
            jnp.where(l_index == 0, sent, value).reshape(local, ny, chunk),
        ],
        axis=2,
    ).reshape(local, width)
    out = (mixed.astype(jnp.float32) + value).astype(bf16)
    return out.reshape(STEPS, rows_dev, width)


def solution(mesh):
    parts = Mesh(mesh.devices.reshape(tuple(SIZES.values())), tuple(SIZES))
    rows = P(None, DP + TENSOR, None)
    placed = (
        rows,
        rows,
        rows,
        P(DP + TENSOR),
        P(DP + TENSOR, None, None),
        P(DP, TENSOR),
        P(TENSOR, None, None),
        P(TENSOR, None, None),
        P(TENSOR, None),
        P(),
        P(DP, TENSOR),
        P(DP, TENSOR),
        P(TENSOR, DP),
    )
    return jax.shard_map(
        shards, mesh=parts, in_specs=placed, out_specs=rows, check_vma=False
    )
```

```python
import math

import jax
import jax.numpy as jnp
from jax import lax
from jax.experimental import pallas as pl
from jax.experimental.pallas import tpu as pltpu
from jax.sharding import Mesh, PartitionSpec as P

NOPE = 128
ROPE = 64
LATENT = 512
VHEAD = 128
STEPS = 2

SIZES = {"y": 4, "l": 2, "z": 4, "x": 4, "c": 2}
DP = ("y", "l")
TENSOR = ("z", "x", "c")
HEADS = ("c", "x", "z")


def shift(value, axis, by):
    size = SIZES[axis]
    return lax.ppermute(value, axis, [(i, (i + by) % size) for i in range(size)])


def nearest_first(size):
    return sorted(range(1, size), key=lambda k: min(k, size - k))


def gather_back(value, axis):
    parts = {0: value}
    for k in nearest_first(SIZES[axis]):
        parts[k] = shift(value, axis, k)
    return jnp.concatenate([parts[k] for k in range(SIZES[axis])], axis=0)


def scatter_back(parts, axis):
    total = parts[0].astype(jnp.float32)
    for by in nearest_first(SIZES[axis]):
        part = parts[SIZES[axis] - by]
        total = total + shift(part, axis, by).astype(jnp.float32)
    return total


def scatter_rows(terms):
    for axis in ("x", "z"):
        rows = terms.shape[0] // SIZES[axis]
        parts = [terms[k * rows : (k + 1) * rows] for k in range(SIZES[axis])]
        terms = scatter_back(parts, axis)
        if axis == "x":
            terms = terms.astype(jnp.bfloat16)
    return terms


def rms_scale(mixed, norm_gain):
    wide = mixed.astype(jnp.float32)
    factor = lax.rsqrt(jnp.mean(wide * wide, axis=-1, keepdims=True) + 1e-06)
    return (wide * factor * norm_gain.astype(jnp.float32)).astype(jnp.bfloat16)


def absorb_rows(kept, away, w_uk, places):
    heads = w_uk.shape[0]
    blocks = places.shape[0]
    rows = kept.shape[0] // blocks
    wide = heads * (LATENT + ROPE)

    def body(places_ref, kept_ref, away_ref, w_ref, out_ref):
        projected = (kept_ref[...] + away_ref[...].astype(jnp.float32)).astype(jnp.bfloat16)
        content, rotary = [], []
        for head in range(heads):
            at = head * (NOPE + ROPE)
            content.append(
                jnp.dot(
                    projected[:, at : at + NOPE], w_ref[head], preferred_element_type=jnp.float32
                )
            )
            rotary.append(projected[:, at + NOPE : at + NOPE + ROPE].astype(jnp.float32))
        query = jnp.concatenate(content + rotary, axis=1)
        for block in range(blocks):
            out_ref[places_ref[block]] = query[block * rows : (block + 1) * rows].astype(
                jnp.bfloat16
            )

    whole = pl.BlockSpec(memory_space=pltpu.VMEM)
    return pl.pallas_call(
        body,
        in_specs=[pl.BlockSpec(memory_space=pltpu.SMEM), whole, whole, whole],
        out_specs=whole,
        out_shape=jax.ShapeDtypeStruct((blocks, rows, wide), jnp.bfloat16),
        cost_estimate=pl.CostEstimate(
            flops=2 * kept.shape[0] * heads * NOPE * LATENT,
            bytes_accessed=6 * kept.size + 2 * w_uk.size + 2 * blocks * rows * wide,
            transcendentals=0,
        ),
        compiler_params=pltpu.CompilerParams(vmem_limit_bytes=32 * 1024 * 1024),
    )(places, kept, away, w_uk)


def attend_rows(query, keys, lengths, turn):
    steps, rows, places, wide = query.shape
    heads = wide // (LATENT + ROPE)
    slots = keys.shape[2] - 128
    scale = (NOPE + ROPE) ** (-0.5)
    per_step = heads * places

    def body(lengths_ref, query_ref, keys_ref, turn_ref, out_ref):
        row = pl.program_id(0)
        content, rotary = [], []
        lane = lax.broadcasted_iota(jnp.int32, (places, 2 * ROPE), 1)
        first_half = lane % ROPE < ROPE // 2
        for step in range(steps):
            for head in range(heads):
                content.append(query_ref[step, 0, :, head * LATENT : (head + 1) * LATENT])
            for pair in range(heads // 2):
                at = heads * LATENT + pair * 2 * ROPE
                value = query_ref[step, 0, :, at : at + 2 * ROPE].astype(jnp.float32)
                other = jnp.where(
                    first_half,
                    pltpu.roll(value, 2 * ROPE - ROPE // 2, 1),
                    pltpu.roll(value, ROPE // 2, 1),
                )
                cosine = turn_ref[0, step, pl.ds(row, 1)]
                sine_part = turn_ref[1, step, pl.ds(row, 1)]
                value = value * cosine + other * sine_part
                rotary.append(jnp.where(lane < ROPE, value, 0.0).astype(jnp.bfloat16))
                rotary.append(jnp.where(lane < ROPE, 0.0, value).astype(jnp.bfloat16))
        content = jnp.concatenate(content, axis=0)
        rotary = jnp.concatenate(rotary, axis=0)
        latents = keys_ref[0, :LATENT]
        turned = keys_ref[0, LATENT:]
        scores = jnp.dot(content, latents, preferred_element_type=jnp.float32)
        scores += jnp.dot(
            rotary, jnp.concatenate([turned, turned], axis=0), preferred_element_type=jnp.float32
        )
        slot = lax.broadcasted_iota(jnp.int32, scores.shape, 1)
        step = lax.broadcasted_iota(jnp.int32, scores.shape, 0) // per_step
        fresh = slot - slots
        seen = (slot < lengths_ref[row]) | ((fresh >= 0) & (fresh <= step))
        scores = jnp.where(seen, scores * scale, -jnp.inf)
        weights = jnp.exp(scores - jnp.max(scores, axis=1, keepdims=True))
        probs = weights / jnp.sum(weights, axis=1, keepdims=True)
        out = lax.dot_general(
            probs.astype(jnp.bfloat16),
            latents,
            (((1,), (1,)), ((), ())),
            preferred_element_type=jnp.float32,
        ).astype(jnp.bfloat16)
        for step in range(steps):
            for head in range(heads):
                at = step * per_step + head * places
                out_ref[step, 0, :, head * LATENT : (head + 1) * LATENT] = out[at : at + places]

    return pl.pallas_call(
        body,
        grid_spec=pltpu.PrefetchScalarGridSpec(
            num_scalar_prefetch=1,
            grid=(rows,),
            in_specs=[
                pl.BlockSpec((steps, 1, places, wide), lambda r, _: (0, r, 0, 0)),
                pl.BlockSpec((1,) + keys.shape[1:], lambda r, _: (r, 0, 0)),
                pl.BlockSpec(turn.shape, lambda r, _: (0, 0, 0, 0)),
            ],
            out_specs=pl.BlockSpec((steps, 1, places, heads * LATENT), lambda r, _: (0, r, 0, 0)),
        ),
        out_shape=jax.ShapeDtypeStruct((steps, rows, places, heads * LATENT), jnp.bfloat16),
        cost_estimate=pl.CostEstimate(
            flops=4 * rows * steps * per_step * LATENT * slots,
            bytes_accessed=4 * query.size + 2 * keys.size,
            transcendentals=rows * steps * per_step * slots,
        ),
        compiler_params=pltpu.CompilerParams(vmem_limit_bytes=32 * 1024 * 1024),
    )(lengths, query, keys, turn)


def shards(
    query_latent,
    fresh_latent,
    stream,
    lengths,
    latent_cache,
    w_qb,
    w_uk,
    w_uv,
    w_o,
    norm_gain,
    w_gate,
    w_up,
    w_down,
):
    bf16 = jnp.bfloat16
    heads_here = w_uk.shape[0]
    rows_dev = lengths.shape[0]
    local = STEPS * rows_dev
    width = stream.shape[-1]
    chunk, units = w_gate.shape
    part = w_qb.shape[0]
    ny, nl, nz, nx, nc = (SIZES[a] for a in ("y", "l", "z", "x", "c"))
    here = {axis: lax.axis_index(axis) for axis in SIZES}
    l_index = here["l"]
    turned = jnp.stack(
        [
            ((here["c"] - c) % nc * nx + (here["x"] - x) % nx) * nz + (here["z"] - z) % nz
            for c in range(nc)
            for x in range(nx)
            for z in range(nz)
        ]
    )

    def by_pair(kept, sent):
        sent = shift(sent, "l", 1)
        return jnp.where(l_index == 0, kept, sent), jnp.where(l_index == 0, sent, kept)

    query_weights = lax.all_gather(w_qb, "y", axis=0, tiled=True)
    split = query_latent.reshape(local, ny, nl, part)
    kept = lax.dynamic_index_in_dim(split, l_index, axis=2, keepdims=False)
    sent = lax.dynamic_index_in_dim(split, 1 - l_index, axis=2, keepdims=False)
    pair = by_pair(kept.reshape(local, ny * part), sent.reshape(local, ny * part))
    everyone = gather_back(jnp.concatenate(pair, axis=0), "z")

    packed = jnp.concatenate([w_gate.T, w_up.T, w_down], axis=0)
    everyone, packed = lax.optimization_barrier((everyone, packed))
    weights = lax.all_gather(packed, "y", axis=1, tiled=True)
    everyone = gather_back(gather_back(everyone, "x"), "c")

    projected = jnp.dot(everyone, query_weights, preferred_element_type=jnp.float32)
    projected = projected.reshape(nc * nx * nz, nl, local, projected.shape[-1])
    kept = jnp.where(l_index == 0, projected[:, 0], projected[:, 1])
    sent = jnp.where(l_index == 0, projected[:, 1], projected[:, 0]).astype(bf16)
    kept, sent = kept.reshape(-1, kept.shape[-1]), sent.reshape(-1, kept.shape[-1])
    query = absorb_rows(kept, shift(sent, "l", 1), w_uk, turned.astype(jnp.int32))
    query = lax.all_to_all(query, HEADS, 0, 0, tiled=True)

    fresh = jnp.transpose(fresh_latent, (1, 2, 0))
    keys = jnp.concatenate(
        [
            jnp.swapaxes(latent_cache, 1, 2),
            jnp.pad(fresh, ((0, 0), (0, 0), (0, 128 - STEPS))),
        ],
        axis=2,
    )
    ladder = jnp.arange(ROPE // 2).astype(jnp.float32)
    frequency = jnp.exp(ladder * (-2.0 * math.log(10000.0) / ROPE))
    position = (lengths[None, :] + jnp.arange(STEPS)[:, None]).astype(jnp.float32)
    angle = position[:, :, None] * frequency
    cosine, sine_part = jnp.cos(angle), jnp.sin(angle)
    turn = jnp.stack(
        [
            jnp.concatenate([cosine, cosine, cosine, cosine], axis=-1),
            jnp.concatenate([-sine_part, sine_part, -sine_part, sine_part], axis=-1),
        ]
    )
    query, keys, turn = lax.optimization_barrier((query, keys, turn))
    query = query.reshape(-1, STEPS, rows_dev, query.shape[-1]).transpose(1, 2, 0, 3)
    attended = attend_rows(query, keys, lengths, turn)
    attended = attended.transpose(2, 0, 1, 3).reshape(-1, local, heads_here * LATENT)

    returned = lax.all_to_all(attended, HEADS, 0, 0, tiled=True)
    returned = returned.reshape(-1, heads_here, LATENT)
    head_values = jnp.einsum(
        "nhc,hcv->nhv", returned, w_uv, preferred_element_type=jnp.float32
    ).astype(bf16)
    head_values = head_values.reshape(nc * nx * nz, local * heads_here * VHEAD)
    head_values = jnp.take(head_values, turned, axis=0, mode="clip").reshape(-1, heads_here * VHEAD)
    terms = jnp.dot(head_values, w_o, preferred_element_type=jnp.float32).astype(bf16)
    half = terms.shape[0] // 2
    terms = terms[:half].astype(jnp.float32) + shift(terms[half:], "c", 1).astype(jnp.float32)
    terms, weights = lax.optimization_barrier((terms.astype(bf16), weights))
    attention_out = scatter_rows(terms)
    mixed = (stream.reshape(local, width).astype(jnp.float32) + attention_out).astype(bf16)
    normed = rms_scale(mixed, norm_gain)

    split = normed.reshape(local, ny, nl, chunk).transpose(2, 0, 1, 3).reshape(nl, local, -1)
    sent = jnp.broadcast_to(split[None], (nz,) + split.shape).reshape(nz * nl, local, -1)
    first = lax.all_to_all(sent, ("z", "l"), 0, 0, tiled=True).reshape(-1, ny * chunk)
    first = lax.optimization_barrier(gather_back(first, "x"))
    second = shift(first, "c", 1)

    def gate_up(rows):
        return lax.dot_general(
            rows,
            weights[: 2 * units],
            (((1,), (1,)), ((), ())),
            preferred_element_type=jnp.float32,
        )

    def down(both, away):
        both = both + away.astype(jnp.float32)
        hidden = (jax.nn.silu(both[:, :units]) * both[:, units:]).astype(bf16)
        return jnp.dot(hidden, weights[2 * units :], preferred_element_type=jnp.float32)

    first, second = gate_up(first), gate_up(second)
    first_away = shift(first.astype(bf16), "l", 1)
    second_away = shift(second.astype(bf16), "l", 1)
    first_away, second_away = lax.optimization_barrier((first_away, second_away))
    away = shift(down(second, second_away).astype(bf16), "c", 1)
    terms = down(first, first_away) + away.astype(jnp.float32)
    rows = terms.shape[0] // nx
    terms = terms.astype(bf16)
    terms = scatter_back([terms[k * rows : (k + 1) * rows] for k in range(nx)], "x").astype(bf16)
    terms = terms.reshape(nz * nl, local, ny * chunk)
    value = lax.all_to_all(terms, ("z", "l"), 0, 0, tiled=True).astype(jnp.float32)
    value = jnp.sum(value.reshape(nz, nl, local, ny, chunk), axis=0)
    value = value.transpose(1, 2, 0, 3).reshape(local, width)
    out = (mixed.astype(jnp.float32) + value).astype(bf16)
    return out.reshape(STEPS, rows_dev, width)


def solution(mesh):
    parts = Mesh(mesh.devices.reshape(tuple(SIZES.values())), tuple(SIZES))
    rows = P(None, DP + TENSOR, None)
    placed = (
        rows,
        rows,
        rows,
        P(DP + TENSOR),
        P(DP + TENSOR, None, None),
        P(DP, TENSOR),
        P(TENSOR, None, None),
        P(TENSOR, None, None),
        P(TENSOR, None),
        P(),
        P(DP, TENSOR),
        P(DP, TENSOR),
        P(TENSOR, DP),
    )
    return jax.shard_map(
        shards, mesh=parts, in_specs=placed, out_specs=rows, check_vma=False
    )
```

```python
import math

import jax
import jax.numpy as jnp
from jax import lax
from jax.experimental import pallas as pl
from jax.experimental.pallas import tpu as pltpu
from jax.sharding import Mesh, PartitionSpec as P

NOPE = 128
ROPE = 64
LATENT = 512
VHEAD = 128
STEPS = 2

SIZES = {"y": 4, "l": 2, "z": 4, "x": 4, "c": 2}
DP = ("y", "l")
TENSOR = ("z", "x", "c")
HEADS = ("c", "x", "z")


def shift(value, axis, by):
    size = SIZES[axis]
    return lax.ppermute(value, axis, [(i, (i + by) % size) for i in range(size)])


def nearest_first(size):
    return sorted(range(1, size), key=lambda k: min(k, size - k))


def gather_back(value, axis):
    parts = {0: value}
    for k in nearest_first(SIZES[axis]):
        parts[k] = shift(value, axis, k)
    return jnp.concatenate([parts[k] for k in range(SIZES[axis])], axis=0)


def scatter_back(parts, axis):
    total = parts[0].astype(jnp.float32)
    for by in nearest_first(SIZES[axis]):
        part = parts[SIZES[axis] - by]
        total = total + shift(part, axis, by).astype(jnp.float32)
    return total


def scatter_rows(terms, carried):
    for axis in ("x", "z"):
        rows = terms.shape[0] // SIZES[axis]
        parts = [terms[k * rows : (k + 1) * rows] for k in range(SIZES[axis])]
        terms = scatter_back(parts, axis)
        if axis == "x":
            terms, carried = lax.optimization_barrier((terms.astype(jnp.bfloat16), carried))
    return terms, carried


def rms_scale(mixed, norm_gain):
    wide = mixed.astype(jnp.float32)
    factor = lax.rsqrt(jnp.mean(wide * wide, axis=-1, keepdims=True) + 1e-06)
    return (wide * factor * norm_gain.astype(jnp.float32)).astype(jnp.bfloat16)


def absorb_rows(kept, away, w_uk, places):
    heads = w_uk.shape[0]
    blocks = places.shape[0]
    rows = kept.shape[0] // blocks
    wide = heads * (LATENT + ROPE)

    def body(places_ref, kept_ref, away_ref, w_ref, out_ref):
        projected = (kept_ref[...] + away_ref[...].astype(jnp.float32)).astype(jnp.bfloat16)
        content, rotary = [], []
        for head in range(heads):
            at = head * (NOPE + ROPE)
            content.append(
                jnp.dot(
                    projected[:, at : at + NOPE], w_ref[head], preferred_element_type=jnp.float32
                )
            )
            rotary.append(projected[:, at + NOPE : at + NOPE + ROPE].astype(jnp.float32))
        query = jnp.concatenate(content + rotary, axis=1)
        for block in range(blocks):
            out_ref[places_ref[block]] = query[block * rows : (block + 1) * rows].astype(
                jnp.bfloat16
            )

    whole = pl.BlockSpec(memory_space=pltpu.VMEM)
    return pl.pallas_call(
        body,
        in_specs=[pl.BlockSpec(memory_space=pltpu.SMEM), whole, whole, whole],
        out_specs=whole,
        out_shape=jax.ShapeDtypeStruct((blocks, rows, wide), jnp.bfloat16),
        cost_estimate=pl.CostEstimate(
            flops=2 * kept.shape[0] * heads * NOPE * LATENT,
            bytes_accessed=6 * kept.size + 2 * w_uk.size + 2 * blocks * rows * wide,
            transcendentals=0,
        ),
        compiler_params=pltpu.CompilerParams(vmem_limit_bytes=32 * 1024 * 1024),
    )(places, kept, away, w_uk)


def attend_rows(query, keys, lengths, turn):
    steps, rows, places, wide = query.shape
    heads = wide // (LATENT + ROPE)
    slots = keys.shape[2] - 128
    scale = (NOPE + ROPE) ** (-0.5)
    per_step = heads * places

    def body(lengths_ref, query_ref, keys_ref, turn_ref, out_ref):
        row = pl.program_id(0)
        content, rotary = [], []
        lane = lax.broadcasted_iota(jnp.int32, (places, 2 * ROPE), 1)
        first_half = lane % ROPE < ROPE // 2
        for step in range(steps):
            for head in range(heads):
                content.append(query_ref[step, 0, :, head * LATENT : (head + 1) * LATENT])
            for pair in range(heads // 2):
                at = heads * LATENT + pair * 2 * ROPE
                value = query_ref[step, 0, :, at : at + 2 * ROPE].astype(jnp.float32)
                other = jnp.where(
                    first_half,
                    pltpu.roll(value, 2 * ROPE - ROPE // 2, 1),
                    pltpu.roll(value, ROPE // 2, 1),
                )
                cosine = turn_ref[0, step, pl.ds(row, 1)]
                sine_part = turn_ref[1, step, pl.ds(row, 1)]
                value = value * cosine + other * sine_part
                rotary.append(jnp.where(lane < ROPE, value, 0.0).astype(jnp.bfloat16))
                rotary.append(jnp.where(lane < ROPE, 0.0, value).astype(jnp.bfloat16))
        content = jnp.concatenate(content, axis=0)
        rotary = jnp.concatenate(rotary, axis=0)
        latents = keys_ref[0, :LATENT]
        turned = keys_ref[0, LATENT:]
        scores = jnp.dot(content, latents, preferred_element_type=jnp.float32)
        scores += jnp.dot(
            rotary, jnp.concatenate([turned, turned], axis=0), preferred_element_type=jnp.float32
        )
        slot = lax.broadcasted_iota(jnp.int32, scores.shape, 1)
        step = lax.broadcasted_iota(jnp.int32, scores.shape, 0) // per_step
        fresh = slot - slots
        seen = (slot < lengths_ref[row]) | ((fresh >= 0) & (fresh <= step))
        scores = jnp.where(seen, scores * scale, -jnp.inf)
        weights = jnp.exp(scores - jnp.max(scores, axis=1, keepdims=True))
        probs = weights / jnp.sum(weights, axis=1, keepdims=True)
        out = lax.dot_general(
            probs.astype(jnp.bfloat16),
            latents,
            (((1,), (1,)), ((), ())),
            preferred_element_type=jnp.float32,
        ).astype(jnp.bfloat16)
        for step in range(steps):
            for head in range(heads):
                at = step * per_step + head * places
                out_ref[step, 0, :, head * LATENT : (head + 1) * LATENT] = out[at : at + places]

    return pl.pallas_call(
        body,
        grid_spec=pltpu.PrefetchScalarGridSpec(
            num_scalar_prefetch=1,
            grid=(rows,),
            in_specs=[
                pl.BlockSpec((steps, 1, places, wide), lambda r, _: (0, r, 0, 0)),
                pl.BlockSpec((1,) + keys.shape[1:], lambda r, _: (r, 0, 0)),
                pl.BlockSpec(turn.shape, lambda r, _: (0, 0, 0, 0)),
            ],
            out_specs=pl.BlockSpec((steps, 1, places, heads * LATENT), lambda r, _: (0, r, 0, 0)),
        ),
        out_shape=jax.ShapeDtypeStruct((steps, rows, places, heads * LATENT), jnp.bfloat16),
        cost_estimate=pl.CostEstimate(
            flops=4 * rows * steps * per_step * LATENT * slots,
            bytes_accessed=4 * query.size + 2 * keys.size,
            transcendentals=rows * steps * per_step * slots,
        ),
        compiler_params=pltpu.CompilerParams(vmem_limit_bytes=32 * 1024 * 1024),
    )(lengths, query, keys, turn)


def shards(
    query_latent,
    fresh_latent,
    stream,
    lengths,
    latent_cache,
    w_qb,
    w_uk,
    w_uv,
    w_o,
    norm_gain,
    w_gate,
    w_up,
    w_down,
):
    bf16 = jnp.bfloat16
    heads_here = w_uk.shape[0]
    rows_dev = lengths.shape[0]
    local = STEPS * rows_dev
    width = stream.shape[-1]
    chunk, units = w_gate.shape
    part = w_qb.shape[0]
    ny, nl, nz, nx, nc = (SIZES[a] for a in ("y", "l", "z", "x", "c"))
    here = {axis: lax.axis_index(axis) for axis in SIZES}
    l_index = here["l"]
    turned = jnp.stack(
        [
            ((here["c"] - c) % nc * nx + (here["x"] - x) % nx) * nz + (here["z"] - z) % nz
            for c in range(nc)
            for x in range(nx)
            for z in range(nz)
        ]
    )

    def by_pair(kept, sent):
        sent = shift(sent, "l", 1)
        return jnp.where(l_index == 0, kept, sent), jnp.where(l_index == 0, sent, kept)

    query_weights = jnp.broadcast_to(w_qb[None], (ny,) + w_qb.shape)
    query_weights = lax.all_to_all(query_weights, "y", 0, 0, tiled=True).reshape(ny * part, -1)
    split = query_latent.reshape(local, ny, nl, part)
    kept = lax.dynamic_index_in_dim(split, l_index, axis=2, keepdims=False)
    sent = lax.dynamic_index_in_dim(split, 1 - l_index, axis=2, keepdims=False)
    pair = by_pair(kept.reshape(local, ny * part), sent.reshape(local, ny * part))
    everyone = gather_back(jnp.concatenate(pair, axis=0), "z")

    packed = jnp.concatenate([w_gate.T, w_up.T, w_down], axis=0)
    everyone, packed = lax.optimization_barrier((everyone, packed))
    near = (shift(packed, "y", 1), shift(packed, "y", -1))
    everyone = gather_back(everyone, "x")
    everyone = gather_back(everyone, "c")

    projected = jnp.dot(everyone, query_weights, preferred_element_type=jnp.float32)
    projected = projected.reshape(nc * nx * nz, nl, local, projected.shape[-1])
    kept = jnp.where(l_index == 0, projected[:, 0], projected[:, 1])
    sent = jnp.where(l_index == 0, projected[:, 1], projected[:, 0]).astype(bf16)
    kept, sent = kept.reshape(-1, kept.shape[-1]), sent.reshape(-1, kept.shape[-1])
    query = absorb_rows(kept, shift(sent, "l", 1), w_uk, turned.astype(jnp.int32))
    query = lax.all_to_all(query, HEADS, 0, 0, tiled=True)

    fresh = jnp.transpose(fresh_latent, (1, 2, 0))
    keys = jnp.concatenate(
        [
            jnp.swapaxes(latent_cache, 1, 2),
            jnp.pad(fresh, ((0, 0), (0, 0), (0, 128 - STEPS))),
        ],
        axis=2,
    )
    ladder = jnp.arange(ROPE // 2).astype(jnp.float32)
    frequency = jnp.exp(ladder * (-2.0 * math.log(10000.0) / ROPE))
    position = (lengths[None, :] + jnp.arange(STEPS)[:, None]).astype(jnp.float32)
    angle = position[:, :, None] * frequency
    cosine, sine_part = jnp.cos(angle), jnp.sin(angle)
    turn = jnp.stack(
        [
            jnp.concatenate([cosine, cosine, cosine, cosine], axis=-1),
            jnp.concatenate([-sine_part, sine_part, -sine_part, sine_part], axis=-1),
        ]
    )
    query, keys, turn = lax.optimization_barrier((query, keys, turn))
    query = query.reshape(-1, STEPS, rows_dev, query.shape[-1]).transpose(1, 2, 0, 3)
    attended = attend_rows(query, keys, lengths, turn)
    attended = attended.transpose(2, 0, 1, 3).reshape(-1, local, heads_here * LATENT)

    returned = lax.all_to_all(attended, HEADS, 0, 0, tiled=True)
    returned, near = lax.optimization_barrier((returned, near))
    onward = (near[0][:units], near[1][units : 2 * units], near[0][2 * units :])
    returned = returned.reshape(-1, heads_here, LATENT)
    head_values = jnp.einsum(
        "nhc,hcv->nhv", returned, w_uv, preferred_element_type=jnp.float32
    ).astype(bf16)
    head_values = head_values.reshape(nc * nx * nz, local * heads_here * VHEAD)
    head_values = jnp.take(head_values, turned, axis=0, mode="clip").reshape(-1, heads_here * VHEAD)
    terms = jnp.dot(head_values, w_o, preferred_element_type=jnp.float32).astype(bf16)
    half = terms.shape[0] // 2
    terms = terms[:half].astype(jnp.float32) + shift(terms[half:], "c", 1).astype(jnp.float32)
    attention_out, onward = scatter_rows(terms.astype(bf16), onward)
    opposite = (shift(onward[0], "y", 1), shift(onward[1], "y", -1))
    opposite_down = shift(onward[2], "y", 1)
    mixed = (stream.reshape(local, width).astype(jnp.float32) + attention_out).astype(bf16)
    normed = rms_scale(mixed, norm_gain)

    back = jnp.stack([(here["y"] - k) % ny for k in range(ny)])
    split = jnp.take(normed.reshape(local, ny, nl, chunk), back, axis=1, mode="clip")
    split = split.transpose(2, 0, 1, 3).reshape(nl, local, -1)
    sent = jnp.broadcast_to(split[None], (nz,) + split.shape).reshape(nz * nl, local, -1)
    first = lax.all_to_all(sent, ("z", "l"), 0, 0, tiled=True).reshape(-1, ny * chunk)
    first, opposite = lax.optimization_barrier((first, opposite))
    first, opposite_down = lax.optimization_barrier((gather_back(first, "x"), opposite_down))
    opposite = jnp.concatenate(opposite, axis=0)
    gate_up_parts = (packed[: 2 * units], near[0][: 2 * units], opposite, near[1][: 2 * units])
    down_parts = (w_down, near[0][2 * units :], opposite_down, near[1][2 * units :])

    def gate_up(rows):
        total = 0.0
        for k, weights in enumerate(gate_up_parts):
            total += lax.dot_general(
                rows[:, k * chunk : (k + 1) * chunk],
                weights,
                (((1,), (1,)), ((), ())),
                preferred_element_type=jnp.float32,
            )
        return total

    def down(both, away):
        both = both + away.astype(jnp.float32)
        hidden = (jax.nn.silu(both[:, :units]) * both[:, units:]).astype(bf16)
        return jnp.concatenate(
            [
                jnp.dot(hidden, weights, preferred_element_type=jnp.float32)
                for weights in down_parts
            ],
            axis=1,
        )

    second = shift(first, "c", 1)
    first = gate_up(first)
    first_away = shift(first.astype(bf16), "l", 1)
    second = gate_up(second)
    second_away = shift(second.astype(bf16), "l", 1)
    first_away, second_away = lax.optimization_barrier((first_away, second_away))
    away = shift(down(second, second_away).astype(bf16), "c", 1)
    terms = down(first, first_away) + away.astype(jnp.float32)
    rows = terms.shape[0] // nx
    terms = terms.astype(bf16)
    terms = scatter_back([terms[k * rows : (k + 1) * rows] for k in range(nx)], "x").astype(bf16)
    terms = terms.reshape(nz * nl, local, ny * chunk)
    value = lax.all_to_all(terms, ("z", "l"), 0, 0, tiled=True).astype(jnp.float32)
    value = jnp.sum(value.reshape(nz, nl, local, ny, chunk), axis=0)
    value = jnp.take(value.transpose(1, 2, 0, 3), back, axis=1, mode="clip").reshape(local, width)
    out = (mixed.astype(jnp.float32) + value).astype(bf16)
    return out.reshape(STEPS, rows_dev, width)


def solution(mesh):
    parts = Mesh(mesh.devices.reshape(tuple(SIZES.values())), tuple(SIZES))
    rows = P(None, DP + TENSOR, None)
    placed = (
        rows,
        rows,
        rows,
        P(DP + TENSOR),
        P(DP + TENSOR, None, None),
        P(DP, TENSOR),
        P(TENSOR, None, None),
        P(TENSOR, None, None),
        P(TENSOR, None),
        P(),
        P(DP, TENSOR),
        P(DP, TENSOR),
        P(TENSOR, DP),
    )
    return jax.shard_map(
        shards, mesh=parts, in_specs=placed, out_specs=rows, check_vma=False
    )
```

```python
import math

import jax
import jax.numpy as jnp
from jax import lax
from jax.experimental import pallas as pl
from jax.experimental.pallas import tpu as pltpu
from jax.sharding import Mesh, PartitionSpec as P

NOPE = 128
ROPE = 64
LATENT = 512
VHEAD = 128
STEPS = 2

SIZES = {"y": 4, "l": 2, "z": 4, "x": 4, "c": 2}
DP = ("y", "l")
TENSOR = ("z", "x", "c")
HEADS = ("c", "x", "z")


def shift(value, axis, by):
    size = SIZES[axis]
    return lax.ppermute(value, axis, [(i, (i + by) % size) for i in range(size)])


def nearest_first(size):
    return sorted(range(1, size), key=lambda k: min(k, size - k))


def gather_back(value, axis):
    parts = {0: value}
    for k in nearest_first(SIZES[axis]):
        parts[k] = shift(value, axis, k)
    return jnp.concatenate([parts[k] for k in range(SIZES[axis])], axis=0)


def scatter_back(parts, axis):
    total = parts[0].astype(jnp.float32)
    for by in nearest_first(SIZES[axis]):
        part = parts[SIZES[axis] - by]
        total = total + shift(part, axis, by).astype(jnp.float32)
    return total


def scatter_rows(terms, carried):
    for axis in ("x", "z"):
        rows = terms.shape[0] // SIZES[axis]
        parts = [terms[k * rows : (k + 1) * rows] for k in range(SIZES[axis])]
        terms = scatter_back(parts, axis)
        if axis == "x":
            terms, carried = lax.optimization_barrier((terms.astype(jnp.bfloat16), carried))
    return terms, carried


def rms_scale(mixed, norm_gain):
    wide = mixed.astype(jnp.float32)
    factor = lax.rsqrt(jnp.mean(wide * wide, axis=-1, keepdims=True) + 1e-06)
    return (wide * factor * norm_gain.astype(jnp.float32)).astype(jnp.bfloat16)


def absorb_rows(kept, away, w_uk, places):
    heads = w_uk.shape[0]
    blocks = places.shape[0]
    rows = kept.shape[0] // blocks
    wide = heads * (LATENT + ROPE)

    def body(places_ref, kept_ref, away_ref, w_ref, out_ref):
        projected = (kept_ref[...] + away_ref[...].astype(jnp.float32)).astype(jnp.bfloat16)
        content, rotary = [], []
        for head in range(heads):
            at = head * (NOPE + ROPE)
            content.append(
                jnp.dot(
                    projected[:, at : at + NOPE], w_ref[head], preferred_element_type=jnp.float32
                )
            )
            rotary.append(projected[:, at + NOPE : at + NOPE + ROPE].astype(jnp.float32))
        query = jnp.concatenate(content + rotary, axis=1)
        for block in range(blocks):
            out_ref[places_ref[block]] = query[block * rows : (block + 1) * rows].astype(
                jnp.bfloat16
            )

    whole = pl.BlockSpec(memory_space=pltpu.VMEM)
    return pl.pallas_call(
        body,
        in_specs=[pl.BlockSpec(memory_space=pltpu.SMEM), whole, whole, whole],
        out_specs=whole,
        out_shape=jax.ShapeDtypeStruct((blocks, rows, wide), jnp.bfloat16),
        cost_estimate=pl.CostEstimate(
            flops=2 * kept.shape[0] * heads * NOPE * LATENT,
            bytes_accessed=6 * kept.size + 2 * w_uk.size + 2 * blocks * rows * wide,
            transcendentals=0,
        ),
        compiler_params=pltpu.CompilerParams(vmem_limit_bytes=32 * 1024 * 1024),
    )(places, kept, away, w_uk)


def attend_rows(query, keys, lengths, turn):
    steps, rows, places, wide = query.shape
    heads = wide // (LATENT + ROPE)
    slots = keys.shape[2] - 128
    scale = (NOPE + ROPE) ** (-0.5)
    per_step = heads * places

    def body(lengths_ref, query_ref, keys_ref, turn_ref, out_ref):
        row = pl.program_id(0)
        content, rotary = [], []
        lane = lax.broadcasted_iota(jnp.int32, (places, 2 * ROPE), 1)
        first_half = lane % ROPE < ROPE // 2
        for step in range(steps):
            for head in range(heads):
                content.append(query_ref[step, 0, :, head * LATENT : (head + 1) * LATENT])
            for pair in range(heads // 2):
                at = heads * LATENT + pair * 2 * ROPE
                value = query_ref[step, 0, :, at : at + 2 * ROPE].astype(jnp.float32)
                other = jnp.where(
                    first_half,
                    pltpu.roll(value, 2 * ROPE - ROPE // 2, 1),
                    pltpu.roll(value, ROPE // 2, 1),
                )
                cosine = turn_ref[0, step, pl.ds(row, 1)]
                sine_part = turn_ref[1, step, pl.ds(row, 1)]
                value = value * cosine + other * sine_part
                rotary.append(jnp.where(lane < ROPE, value, 0.0).astype(jnp.bfloat16))
                rotary.append(jnp.where(lane < ROPE, 0.0, value).astype(jnp.bfloat16))
        content = jnp.concatenate(content, axis=0)
        rotary = jnp.concatenate(rotary, axis=0)
        latents = keys_ref[0, :LATENT]
        turned = keys_ref[0, LATENT:]
        scores = jnp.dot(content, latents, preferred_element_type=jnp.float32)
        scores += jnp.dot(
            rotary, jnp.concatenate([turned, turned], axis=0), preferred_element_type=jnp.float32
        )
        slot = lax.broadcasted_iota(jnp.int32, scores.shape, 1)
        step = lax.broadcasted_iota(jnp.int32, scores.shape, 0) // per_step
        fresh = slot - slots
        seen = (slot < lengths_ref[row]) | ((fresh >= 0) & (fresh <= step))
        scores = jnp.where(seen, scores * scale, -jnp.inf)
        weights = jnp.exp(scores - jnp.max(scores, axis=1, keepdims=True))
        probs = weights / jnp.sum(weights, axis=1, keepdims=True)
        out = lax.dot_general(
            probs.astype(jnp.bfloat16),
            latents,
            (((1,), (1,)), ((), ())),
            preferred_element_type=jnp.float32,
        ).astype(jnp.bfloat16)
        for step in range(steps):
            for head in range(heads):
                at = step * per_step + head * places
                out_ref[step, 0, :, head * LATENT : (head + 1) * LATENT] = out[at : at + places]

    return pl.pallas_call(
        body,
        grid_spec=pltpu.PrefetchScalarGridSpec(
            num_scalar_prefetch=1,
            grid=(rows,),
            in_specs=[
                pl.BlockSpec((steps, 1, places, wide), lambda r, _: (0, r, 0, 0)),
                pl.BlockSpec((1,) + keys.shape[1:], lambda r, _: (r, 0, 0)),
                pl.BlockSpec(turn.shape, lambda r, _: (0, 0, 0, 0)),
            ],
            out_specs=pl.BlockSpec((steps, 1, places, heads * LATENT), lambda r, _: (0, r, 0, 0)),
        ),
        out_shape=jax.ShapeDtypeStruct((steps, rows, places, heads * LATENT), jnp.bfloat16),
        cost_estimate=pl.CostEstimate(
            flops=4 * rows * steps * per_step * LATENT * slots,
            bytes_accessed=4 * query.size + 2 * keys.size,
            transcendentals=rows * steps * per_step * slots,
        ),
        compiler_params=pltpu.CompilerParams(vmem_limit_bytes=32 * 1024 * 1024),
    )(lengths, query, keys, turn)


def shards(
    query_latent,
    fresh_latent,
    stream,
    lengths,
    latent_cache,
    w_qb,
    w_uk,
    w_uv,
    w_o,
    norm_gain,
    w_gate,
    w_up,
    w_down,
):
    bf16 = jnp.bfloat16
    heads_here = w_uk.shape[0]
    rows_dev = lengths.shape[0]
    local = STEPS * rows_dev
    width = stream.shape[-1]
    chunk, units = w_gate.shape
    part = w_qb.shape[0]
    ny, nl, nz, nx, nc = (SIZES[a] for a in ("y", "l", "z", "x", "c"))
    here = {axis: lax.axis_index(axis) for axis in SIZES}
    l_index = here["l"]
    turned = jnp.stack(
        [
            ((here["c"] - c) % nc * nx + (here["x"] - x) % nx) * nz + (here["z"] - z) % nz
            for c in range(nc)
            for x in range(nx)
            for z in range(nz)
        ]
    )

    def by_pair(kept, sent):
        sent = shift(sent, "l", 1)
        return jnp.where(l_index == 0, kept, sent), jnp.where(l_index == 0, sent, kept)

    query_weights = jnp.broadcast_to(w_qb[None], (ny,) + w_qb.shape)
    query_weights = lax.all_to_all(query_weights, "y", 0, 0, tiled=True).reshape(ny * part, -1)
    split = query_latent.reshape(local, ny, nl, part)
    kept = lax.dynamic_index_in_dim(split, l_index, axis=2, keepdims=False)
    sent = lax.dynamic_index_in_dim(split, 1 - l_index, axis=2, keepdims=False)
    pair = by_pair(kept.reshape(local, ny * part), sent.reshape(local, ny * part))
    everyone = gather_back(jnp.concatenate(pair, axis=0), "z")

    packed = jnp.concatenate([w_gate.T, w_up.T, w_down], axis=0)
    everyone, packed = lax.optimization_barrier((everyone, packed))
    near = (shift(packed, "y", 1), shift(packed, "y", -1))
    everyone = gather_back(everyone, "x")
    everyone = gather_back(everyone, "c")

    projected = jnp.dot(everyone, query_weights, preferred_element_type=jnp.float32)
    projected = projected.reshape(nc * nx * nz, nl, local, projected.shape[-1])
    kept = jnp.where(l_index == 0, projected[:, 0], projected[:, 1])
    sent = jnp.where(l_index == 0, projected[:, 1], projected[:, 0]).astype(bf16)
    kept, sent = kept.reshape(-1, kept.shape[-1]), sent.reshape(-1, kept.shape[-1])
    query = absorb_rows(kept, shift(sent, "l", 1), w_uk, turned.astype(jnp.int32))
    query = lax.all_to_all(query, HEADS, 0, 0, tiled=True)

    fresh = jnp.transpose(fresh_latent, (1, 2, 0))
    keys = jnp.concatenate(
        [
            jnp.swapaxes(latent_cache, 1, 2),
            jnp.pad(fresh, ((0, 0), (0, 0), (0, 128 - STEPS))),
        ],
        axis=2,
    )
    ladder = jnp.arange(ROPE // 2).astype(jnp.float32)
    frequency = jnp.exp(ladder * (-2.0 * math.log(10000.0) / ROPE))
    position = (lengths[None, :] + jnp.arange(STEPS)[:, None]).astype(jnp.float32)
    angle = position[:, :, None] * frequency
    cosine, sine_part = jnp.cos(angle), jnp.sin(angle)
    turn = jnp.stack(
        [
            jnp.concatenate([cosine, cosine, cosine, cosine], axis=-1),
            jnp.concatenate([-sine_part, sine_part, -sine_part, sine_part], axis=-1),
        ]
    )
    query, keys, turn = lax.optimization_barrier((query, keys, turn))
    query = query.reshape(-1, STEPS, rows_dev, query.shape[-1]).transpose(1, 2, 0, 3)
    attended = attend_rows(query, keys, lengths, turn)
    attended = attended.transpose(2, 0, 1, 3).reshape(-1, local, heads_here * LATENT)

    returned = lax.all_to_all(attended, HEADS, 0, 0, tiled=True)
    returned, near = lax.optimization_barrier((returned, near))
    onward = (near[0][:units], near[1][units : 2 * units])
    returned = returned.reshape(-1, heads_here, LATENT)
    head_values = jnp.einsum(
        "nhc,hcv->nhv", returned, w_uv, preferred_element_type=jnp.float32
    ).astype(bf16)
    head_values = head_values.reshape(nc * nx * nz, local * heads_here * VHEAD)
    head_values = jnp.take(head_values, turned, axis=0, mode="clip").reshape(-1, heads_here * VHEAD)
    terms = jnp.dot(head_values, w_o, preferred_element_type=jnp.float32).astype(bf16)
    half = terms.shape[0] // 2
    terms = terms[:half].astype(jnp.float32) + shift(terms[half:], "c", 1).astype(jnp.float32)
    attention_out, onward = scatter_rows(terms.astype(bf16), onward)
    opposite = (shift(onward[0], "y", 1), shift(onward[1], "y", -1))
    opposite_down = shift(near[0][2 * units :], "y", 1)
    mixed = (stream.reshape(local, width).astype(jnp.float32) + attention_out).astype(bf16)
    normed = rms_scale(mixed, norm_gain)

    back = jnp.stack([(here["y"] - k) % ny for k in range(ny)])
    split = jnp.take(normed.reshape(local, ny, nl, chunk), back, axis=1, mode="clip")
    split = split.transpose(2, 0, 1, 3).reshape(nl, local, -1)
    sent = jnp.broadcast_to(split[None], (nz,) + split.shape).reshape(nz * nl, local, -1)
    first = lax.all_to_all(sent, ("z", "l"), 0, 0, tiled=True).reshape(-1, ny * chunk)
    first, opposite = lax.optimization_barrier((first, opposite))
    first, opposite_down = lax.optimization_barrier((gather_back(first, "x"), opposite_down))
    opposite = jnp.concatenate(opposite, axis=0)
    gate_up_parts = (packed[: 2 * units], near[0][: 2 * units], opposite, near[1][: 2 * units])
    down_parts = (w_down, near[0][2 * units :], opposite_down, near[1][2 * units :])

    def gate_up(rows):
        total = 0.0
        for k, weights in enumerate(gate_up_parts):
            total += lax.dot_general(
                rows[:, k * chunk : (k + 1) * chunk],
                weights,
                (((1,), (1,)), ((), ())),
                preferred_element_type=jnp.float32,
            )
        return total

    def down(both, away):
        both = both + away.astype(jnp.float32)
        hidden = (jax.nn.silu(both[:, :units]) * both[:, units:]).astype(bf16)
        return jnp.concatenate(
            [
                jnp.dot(hidden, weights, preferred_element_type=jnp.float32)
                for weights in down_parts
            ],
            axis=1,
        )

    second = shift(first, "c", 1)
    first = gate_up(first)
    first_away = shift(first.astype(bf16), "l", 1)
    second = gate_up(second)
    second_away = shift(second.astype(bf16), "l", 1)
    first_away, second_away = lax.optimization_barrier((first_away, second_away))
    away = shift(down(second, second_away).astype(bf16), "c", 1)
    terms = down(first, first_away) + away.astype(jnp.float32)
    rows = terms.shape[0] // nx
    terms = terms.astype(bf16)
    terms = scatter_back([terms[k * rows : (k + 1) * rows] for k in range(nx)], "x").astype(bf16)
    terms = terms.reshape(nz * nl, local, ny * chunk)
    value = lax.all_to_all(terms, ("z", "l"), 0, 0, tiled=True).astype(jnp.float32)
    value = jnp.sum(value.reshape(nz, nl, local, ny, chunk), axis=0)
    value = jnp.take(value.transpose(1, 2, 0, 3), back, axis=1, mode="clip").reshape(local, width)
    out = (mixed.astype(jnp.float32) + value).astype(bf16)
    return out.reshape(STEPS, rows_dev, width)


def solution(mesh):
    parts = Mesh(mesh.devices.reshape(tuple(SIZES.values())), tuple(SIZES))
    rows = P(None, DP + TENSOR, None)
    placed = (
        rows,
        rows,
        rows,
        P(DP + TENSOR),
        P(DP + TENSOR, None, None),
        P(DP, TENSOR),
        P(TENSOR, None, None),
        P(TENSOR, None, None),
        P(TENSOR, None),
        P(),
        P(DP, TENSOR),
        P(DP, TENSOR),
        P(TENSOR, DP),
    )
    return jax.shard_map(
        shards, mesh=parts, in_specs=placed, out_specs=rows, check_vma=False
    )
```

```python
import math

import jax
import jax.numpy as jnp
from jax import lax
from jax.experimental import pallas as pl
from jax.experimental.pallas import tpu as pltpu
from jax.sharding import Mesh, PartitionSpec as P

NOPE = 128
ROPE = 64
LATENT = 512
VHEAD = 128
STEPS = 2

SIZES = {"y": 4, "l": 2, "z": 4, "x": 4, "c": 2}
DP = ("y", "l")
TENSOR = ("z", "x", "c")
HEADS = ("c", "x", "z")


def shift(value, axis, by):
    size = SIZES[axis]
    return lax.ppermute(value, axis, [(i, (i + by) % size) for i in range(size)])


def nearest_first(size):
    return sorted(range(1, size), key=lambda k: min(k, size - k))


def gather_back(value, axis):
    parts = {0: value}
    for k in nearest_first(SIZES[axis]):
        parts[k] = shift(value, axis, k)
    return jnp.concatenate([parts[k] for k in range(SIZES[axis])], axis=0)


def scatter_back(parts, axis):
    total = parts[0].astype(jnp.float32)
    for by in nearest_first(SIZES[axis]):
        part = parts[SIZES[axis] - by]
        total = total + shift(part, axis, by).astype(jnp.float32)
    return total


def scatter_rows(terms, carried):
    for axis in ("x", "z"):
        rows = terms.shape[0] // SIZES[axis]
        parts = [terms[k * rows : (k + 1) * rows] for k in range(SIZES[axis])]
        terms = scatter_back(parts, axis)
        if axis == "x":
            terms, carried = lax.optimization_barrier((terms.astype(jnp.bfloat16), carried))
    return terms, carried


def rms_scale(mixed, norm_gain):
    wide = mixed.astype(jnp.float32)
    factor = lax.rsqrt(jnp.mean(wide * wide, axis=-1, keepdims=True) + 1e-06)
    return (wide * factor * norm_gain.astype(jnp.float32)).astype(jnp.bfloat16)


def absorb_rows(kept, away, w_uk, places):
    heads = w_uk.shape[0]
    blocks = places.shape[0]
    rows = kept.shape[0] // blocks
    wide = heads * (LATENT + ROPE)

    def body(places_ref, kept_ref, away_ref, w_ref, out_ref):
        projected = (kept_ref[...] + away_ref[...].astype(jnp.float32)).astype(jnp.bfloat16)
        content, rotary = [], []
        for head in range(heads):
            at = head * (NOPE + ROPE)
            content.append(
                jnp.dot(
                    projected[:, at : at + NOPE], w_ref[head], preferred_element_type=jnp.float32
                )
            )
            rotary.append(projected[:, at + NOPE : at + NOPE + ROPE].astype(jnp.float32))
        query = jnp.concatenate(content + rotary, axis=1)
        for block in range(blocks):
            out_ref[places_ref[block]] = query[block * rows : (block + 1) * rows].astype(
                jnp.bfloat16
            )

    whole = pl.BlockSpec(memory_space=pltpu.VMEM)
    return pl.pallas_call(
        body,
        in_specs=[pl.BlockSpec(memory_space=pltpu.SMEM), whole, whole, whole],
        out_specs=whole,
        out_shape=jax.ShapeDtypeStruct((blocks, rows, wide), jnp.bfloat16),
        cost_estimate=pl.CostEstimate(
            flops=2 * kept.shape[0] * heads * NOPE * LATENT,
            bytes_accessed=6 * kept.size + 2 * w_uk.size + 2 * blocks * rows * wide,
            transcendentals=0,
        ),
        compiler_params=pltpu.CompilerParams(vmem_limit_bytes=32 * 1024 * 1024),
    )(places, kept, away, w_uk)


def attend_rows(query, keys, lengths, turn):
    steps, rows, places, wide = query.shape
    heads = wide // (LATENT + ROPE)
    slots = keys.shape[2] - 128
    scale = (NOPE + ROPE) ** (-0.5)
    per_step = heads * places

    def body(lengths_ref, query_ref, keys_ref, turn_ref, out_ref):
        row = pl.program_id(0)
        content, rotary = [], []
        lane = lax.broadcasted_iota(jnp.int32, (places, 2 * ROPE), 1)
        first_half = lane % ROPE < ROPE // 2
        for step in range(steps):
            for head in range(heads):
                content.append(query_ref[step, 0, :, head * LATENT : (head + 1) * LATENT])
            for pair in range(heads // 2):
                at = heads * LATENT + pair * 2 * ROPE
                value = query_ref[step, 0, :, at : at + 2 * ROPE].astype(jnp.float32)
                other = jnp.where(
                    first_half,
                    pltpu.roll(value, 2 * ROPE - ROPE // 2, 1),
                    pltpu.roll(value, ROPE // 2, 1),
                )
                cosine = turn_ref[0, step, pl.ds(row, 1)]
                sine_part = turn_ref[1, step, pl.ds(row, 1)]
                value = value * cosine + other * sine_part
                rotary.append(jnp.where(lane < ROPE, value, 0.0).astype(jnp.bfloat16))
                rotary.append(jnp.where(lane < ROPE, 0.0, value).astype(jnp.bfloat16))
        content = jnp.concatenate(content, axis=0)
        rotary = jnp.concatenate(rotary, axis=0)
        latents = keys_ref[0, :LATENT]
        turned = keys_ref[0, LATENT:]
        scores = jnp.dot(content, latents, preferred_element_type=jnp.float32)
        scores += jnp.dot(
            rotary, jnp.concatenate([turned, turned], axis=0), preferred_element_type=jnp.float32
        )
        slot = lax.broadcasted_iota(jnp.int32, scores.shape, 1)
        step = lax.broadcasted_iota(jnp.int32, scores.shape, 0) // per_step
        fresh = slot - slots
        seen = (slot < lengths_ref[row]) | ((fresh >= 0) & (fresh <= step))
        scores = jnp.where(seen, scores * scale, -jnp.inf)
        weights = jnp.exp(scores - jnp.max(scores, axis=1, keepdims=True))
        probs = weights / jnp.sum(weights, axis=1, keepdims=True)
        out = lax.dot_general(
            probs.astype(jnp.bfloat16),
            latents,
            (((1,), (1,)), ((), ())),
            preferred_element_type=jnp.float32,
        ).astype(jnp.bfloat16)
        for step in range(steps):
            for head in range(heads):
                at = step * per_step + head * places
                out_ref[step, 0, :, head * LATENT : (head + 1) * LATENT] = out[at : at + places]

    return pl.pallas_call(
        body,
        grid_spec=pltpu.PrefetchScalarGridSpec(
            num_scalar_prefetch=1,
            grid=(rows,),
            in_specs=[
                pl.BlockSpec((steps, 1, places, wide), lambda r, _: (0, r, 0, 0)),
                pl.BlockSpec((1,) + keys.shape[1:], lambda r, _: (r, 0, 0)),
                pl.BlockSpec(turn.shape, lambda r, _: (0, 0, 0, 0)),
            ],
            out_specs=pl.BlockSpec((steps, 1, places, heads * LATENT), lambda r, _: (0, r, 0, 0)),
        ),
        out_shape=jax.ShapeDtypeStruct((steps, rows, places, heads * LATENT), jnp.bfloat16),
        cost_estimate=pl.CostEstimate(
            flops=4 * rows * steps * per_step * LATENT * slots,
            bytes_accessed=4 * query.size + 2 * keys.size,
            transcendentals=rows * steps * per_step * slots,
        ),
        compiler_params=pltpu.CompilerParams(vmem_limit_bytes=32 * 1024 * 1024),
    )(lengths, query, keys, turn)


def shards(
    query_latent,
    fresh_latent,
    stream,
    lengths,
    latent_cache,
    w_qb,
    w_uk,
    w_uv,
    w_o,
    norm_gain,
    w_gate,
    w_up,
    w_down,
):
    bf16 = jnp.bfloat16
    heads_here = w_uk.shape[0]
    rows_dev = lengths.shape[0]
    local = STEPS * rows_dev
    width = stream.shape[-1]
    chunk, units = w_gate.shape
    part = w_qb.shape[0]
    ny, nl, nz, nx, nc = (SIZES[a] for a in ("y", "l", "z", "x", "c"))
    here = {axis: lax.axis_index(axis) for axis in SIZES}
    l_index = here["l"]
    turned = jnp.stack(
        [
            ((here["c"] - c) % nc * nx + (here["x"] - x) % nx) * nz + (here["z"] - z) % nz
            for c in range(nc)
            for x in range(nx)
            for z in range(nz)
        ]
    )

    def by_pair(kept, sent):
        sent = shift(sent, "l", 1)
        return jnp.where(l_index == 0, kept, sent), jnp.where(l_index == 0, sent, kept)

    split = query_latent.reshape(local, ny, nl, part)
    kept = lax.dynamic_index_in_dim(split, l_index, axis=2, keepdims=False)
    sent = lax.dynamic_index_in_dim(split, 1 - l_index, axis=2, keepdims=False)
    pair = by_pair(kept.reshape(local, ny * part), sent.reshape(local, ny * part))
    pair, w_qb = lax.optimization_barrier((jnp.concatenate(pair, axis=0), w_qb))
    everyone = gather_back(pair, "z")
    query_weights = jnp.broadcast_to(w_qb[None], (ny,) + w_qb.shape)
    query_weights = lax.all_to_all(query_weights, "y", 0, 0, tiled=True).reshape(ny * part, -1)

    packed = jnp.concatenate([w_gate.T, w_up.T, w_down], axis=0)
    everyone, packed = lax.optimization_barrier((everyone, packed))
    near = (shift(packed, "y", 1), shift(packed, "y", -1))
    everyone = gather_back(everyone, "x")
    everyone = gather_back(everyone, "c")

    projected = jnp.dot(everyone, query_weights, preferred_element_type=jnp.float32)
    projected = projected.reshape(nc * nx * nz, nl, local, projected.shape[-1])
    kept = jnp.where(l_index == 0, projected[:, 0], projected[:, 1])
    sent = jnp.where(l_index == 0, projected[:, 1], projected[:, 0]).astype(bf16)
    kept, sent = kept.reshape(-1, kept.shape[-1]), sent.reshape(-1, kept.shape[-1])
    query = absorb_rows(kept, shift(sent, "l", 1), w_uk, turned.astype(jnp.int32))
    query = lax.all_to_all(query, HEADS, 0, 0, tiled=True)

    fresh = jnp.transpose(fresh_latent, (1, 2, 0))
    keys = jnp.concatenate(
        [
            jnp.swapaxes(latent_cache, 1, 2),
            jnp.pad(fresh, ((0, 0), (0, 0), (0, 128 - STEPS))),
        ],
        axis=2,
    )
    ladder = jnp.arange(ROPE // 2).astype(jnp.float32)
    frequency = jnp.exp(ladder * (-2.0 * math.log(10000.0) / ROPE))
    position = (lengths[None, :] + jnp.arange(STEPS)[:, None]).astype(jnp.float32)
    angle = position[:, :, None] * frequency
    cosine, sine_part = jnp.cos(angle), jnp.sin(angle)
    turn = jnp.stack(
        [
            jnp.concatenate([cosine, cosine, cosine, cosine], axis=-1),
            jnp.concatenate([-sine_part, sine_part, -sine_part, sine_part], axis=-1),
        ]
    )
    query, keys, turn = lax.optimization_barrier((query, keys, turn))
    query = query.reshape(-1, STEPS, rows_dev, query.shape[-1]).transpose(1, 2, 0, 3)
    attended = attend_rows(query, keys, lengths, turn)
    attended = attended.transpose(2, 0, 1, 3).reshape(-1, local, heads_here * LATENT)

    returned = lax.all_to_all(attended, HEADS, 0, 0, tiled=True)
    returned, near = lax.optimization_barrier((returned, near))
    onward = (near[0][:units], near[1][units : 2 * units])
    returned = returned.reshape(-1, heads_here, LATENT)
    head_values = jnp.einsum(
        "nhc,hcv->nhv", returned, w_uv, preferred_element_type=jnp.float32
    ).astype(bf16)
    head_values = head_values.reshape(nc * nx * nz, local * heads_here * VHEAD)
    head_values = jnp.take(head_values, turned, axis=0, mode="clip").reshape(-1, heads_here * VHEAD)
    terms = jnp.dot(head_values, w_o, preferred_element_type=jnp.float32).astype(bf16)
    half = terms.shape[0] // 2
    terms = terms[:half].astype(jnp.float32) + shift(terms[half:], "c", 1).astype(jnp.float32)
    attention_out, onward = scatter_rows(terms.astype(bf16), onward)
    opposite = (shift(onward[0], "y", 1), shift(onward[1], "y", -1))
    opposite_down = shift(near[0][2 * units :], "y", 1)
    mixed = (stream.reshape(local, width).astype(jnp.float32) + attention_out).astype(bf16)
    normed = rms_scale(mixed, norm_gain)

    back = jnp.stack([(here["y"] - k) % ny for k in range(ny)])
    split = jnp.take(normed.reshape(local, ny, nl, chunk), back, axis=1, mode="clip")
    split = split.transpose(2, 0, 1, 3).reshape(nl, local, -1)
    sent = jnp.broadcast_to(split[None], (nz,) + split.shape).reshape(nz * nl, local, -1)
    first = lax.all_to_all(sent, ("z", "l"), 0, 0, tiled=True).reshape(-1, ny * chunk)
    first, opposite = lax.optimization_barrier((first, opposite))
    first, opposite_down = lax.optimization_barrier((gather_back(first, "x"), opposite_down))
    opposite = jnp.concatenate(opposite, axis=0)
    gate_up_parts = (packed[: 2 * units], near[0][: 2 * units], opposite, near[1][: 2 * units])
    down_parts = (w_down, near[0][2 * units :], opposite_down, near[1][2 * units :])

    def gate_up(rows):
        total = 0.0
        for k, weights in enumerate(gate_up_parts):
            total += lax.dot_general(
                rows[:, k * chunk : (k + 1) * chunk],
                weights,
                (((1,), (1,)), ((), ())),
                preferred_element_type=jnp.float32,
            )
        return total

    def down(both, away):
        both = both + away.astype(jnp.float32)
        hidden = (jax.nn.silu(both[:, :units]) * both[:, units:]).astype(bf16)
        return jnp.concatenate(
            [
                jnp.dot(hidden, weights, preferred_element_type=jnp.float32)
                for weights in down_parts
            ],
            axis=1,
        )

    second = shift(first, "c", 1)
    first = gate_up(first)
    first_away = shift(first.astype(bf16), "l", 1)
    second = gate_up(second)
    second_away = shift(second.astype(bf16), "l", 1)
    first_away, second_away = lax.optimization_barrier((first_away, second_away))
    away = shift(down(second, second_away).astype(bf16), "c", 1)
    terms = down(first, first_away) + away.astype(jnp.float32)
    rows = terms.shape[0] // nx
    terms = terms.astype(bf16)
    terms = scatter_back([terms[k * rows : (k + 1) * rows] for k in range(nx)], "x").astype(bf16)
    terms = terms.reshape(nz * nl, local, ny * chunk)
    value = lax.all_to_all(terms, ("z", "l"), 0, 0, tiled=True).astype(jnp.float32)
    value = jnp.sum(value.reshape(nz, nl, local, ny, chunk), axis=0)
    value = jnp.take(value.transpose(1, 2, 0, 3), back, axis=1, mode="clip").reshape(local, width)
    out = (mixed.astype(jnp.float32) + value).astype(bf16)
    return out.reshape(STEPS, rows_dev, width)


def solution(mesh):
    parts = Mesh(mesh.devices.reshape(tuple(SIZES.values())), tuple(SIZES))
    rows = P(None, DP + TENSOR, None)
    placed = (
        rows,
        rows,
        rows,
        P(DP + TENSOR),
        P(DP + TENSOR, None, None),
        P(DP, TENSOR),
        P(TENSOR, None, None),
        P(TENSOR, None, None),
        P(TENSOR, None),
        P(),
        P(DP, TENSOR),
        P(DP, TENSOR),
        P(TENSOR, DP),
    )
    return jax.shard_map(
        shards, mesh=parts, in_specs=placed, out_specs=rows, check_vma=False
    )
```
